256 devices in a mesh: dp: 16 (over z_lo, x), ctx: 16 (over y, z_hi, core).
Axes of the slice: x: 4, y: 4, z: 8 (z_hi: 2, z_lo: 4; z = z_hi * 4 + z_lo), core: 2. Of those that a mesh axis runs over, the one named last changes fastest.
Arguments:
- queries: bfloat16 [16, 2048, 4096], P('dp', 'ctx'), may hold values from -6 to 6
- key_rows: bfloat16 [16, 2048, 4096], P('dp', 'ctx'), may hold values from -6 to 6
- value_rows: bfloat16 [16, 2048, 4096], P('dp', 'ctx'), may hold values from -6 to 6
- log_decay: float32 [16, 2048, 32], P('dp', 'ctx'), may hold values from -2 to 0, as said below
- out_weight: bfloat16 [4096, 3072], P('dp'), may hold values from -0.09375 to 0.09375
- out_grad: bfloat16 [16, 2048, 3072], P('dp', 'ctx'), may hold values from -6 to 6
Outputs:
- projected: bfloat16 [16, 2048, 3072], P('dp', 'ctx')
- query_grad: bfloat16 [16, 2048, 4096], P('dp', 'ctx')
- key_grad: bfloat16 [16, 2048, 4096], P('dp', 'ctx')
- value_grad: bfloat16 [16, 2048, 4096], P('dp', 'ctx')
The draws below stay inside these ranges and needn't reach their ends.
Inputs may be any that keep to these rules, and one draw needn't show every extreme that they name: `log_decay`: every entry is negative.
All inputs are finite; a program needn't handle non-finite values.
Results may differ from the reference program's by a relative error of at most 0.015.
Values may be sent and summed in bfloat16 or wider, within the bound.
No kernel may reach another device: no remote copies, remote signals or barrier semaphores. Data moves between devices by JAX's collectives and lax.ppermute only.
A program may use at most 256 MiB of HBM per device.

```python
import math
import jax
import jax.numpy as jnp
from jax import lax

D = 3072
HEAD_TOTAL = 32
DH = 128
TOK_DEV = 128
SEQUENCE_LENGTH = 2048
SEQUENCE_COUNT = 16


def draw_log_decay(key, part):
    key = jax.random.fold_in(key, 7)
    random_subkeys = jax.random.split(key, 6)
    fast_share = 0.5
    fast_heads = jax.random.bernoulli(random_subkeys[0], fast_share, (SEQUENCE_COUNT, 1, HEAD_TOTAL))
    fast_rate = jnp.exp(jax.random.uniform(random_subkeys[1], (SEQUENCE_COUNT, 1, HEAD_TOTAL), jnp.float32, math.log(1.0 / 50.0), math.log(1.0 / 30.0)))
    slow_rate = jnp.exp(jax.random.uniform(random_subkeys[2], (SEQUENCE_COUNT, 1, HEAD_TOTAL), jnp.float32, math.log(0.02 / SEQUENCE_LENGTH), math.log(0.2 / SEQUENCE_LENGTH)))
    base_rate = jnp.where(fast_heads, fast_rate, slow_rate)
    blocks = SEQUENCE_LENGTH // TOK_DEV
    factor = jnp.exp(jax.random.uniform(random_subkeys[3], (SEQUENCE_COUNT, blocks, 1, HEAD_TOTAL), jnp.float32, math.log(0.6), math.log(1.8)))
    block_rates = base_rate[:, :, None, :] * factor
    decay_rates = jnp.broadcast_to(block_rates, (SEQUENCE_COUNT, blocks, TOK_DEV, HEAD_TOTAL)).reshape(SEQUENCE_COUNT, SEQUENCE_LENGTH, HEAD_TOTAL)
    spike_position = jax.random.randint(random_subkeys[4], (SEQUENCE_COUNT, 1, 3, HEAD_TOTAL), 0, SEQUENCE_LENGTH)
    spike_retained = jax.random.uniform(random_subkeys[5], (SEQUENCE_COUNT, 1, 3, HEAD_TOTAL), jnp.float32, 0.55, 0.8)
    token_places = jnp.arange(SEQUENCE_LENGTH)[None, :, None, None]
    spike_events = jnp.sum(jnp.where(token_places == spike_position, jnp.log(spike_retained), 0.0), axis=2)
    return (spike_events - decay_rates).astype(jnp.float32)


def steps_of(own_key, dims, cuts, low, top_value):
    factor_of = 1.0
    for axis_at, blocks in cuts:
        heights = jax.random.uniform(jax.random.fold_in(jax.random.fold_in(own_key, 6), axis_at), (blocks,), jnp.float32, low / len(cuts), top_value / len(cuts))
        factor_of = factor_of * jnp.repeat(jnp.exp(heights), dims[axis_at] // blocks).reshape((-1,) + (1,) * (len(dims) - 1 - axis_at))
    return factor_of


def scatter_about(stream_key, shape, spread, bound, cuts=(), dtype=jnp.bfloat16):
    gain = steps_of(stream_key, shape, cuts, -0.22, 0.18) if cuts else 1.0
    entries = jax.random.normal(stream_key, shape, jnp.float32) * spread * gain
    return jnp.minimum(jnp.maximum(entries, -bound), bound).astype(dtype)


def setup_inputs(seed: int = 0) -> dict:
    streams_of = jax.random.split(jax.random.key(seed), 7)
    queries = scatter_about(streams_of[0], (SEQUENCE_COUNT, SEQUENCE_LENGTH, HEAD_TOTAL * DH), 1.0, 6.0, ((0, 16), (1, 16)))
    key_rows = scatter_about(streams_of[1], (SEQUENCE_COUNT, SEQUENCE_LENGTH, HEAD_TOTAL * DH), 1.0, 6.0, ((0, 16), (1, 16)))
    value_rows = scatter_about(streams_of[2], (SEQUENCE_COUNT, SEQUENCE_LENGTH, HEAD_TOTAL * DH), 1.0, 6.0, ((0, 16), (1, 16)))
    log_decay = draw_log_decay(jax.random.fold_in(streams_of[6], 71), 0)
    out_weight = scatter_about(streams_of[4], (HEAD_TOTAL * DH, D), (HEAD_TOTAL * DH) ** -0.5, 0.09375, ((0, 16),))
    out_grad = scatter_about(streams_of[5], (SEQUENCE_COUNT, SEQUENCE_LENGTH, D), 1.0, 6.0, ((0, 16), (1, 16)))
    return dict(queries=queries, key_rows=key_rows, value_rows=value_rows, log_decay=log_decay, out_weight=out_weight, out_grad=out_grad)


HIGH = lax.Precision.HIGHEST


def local_decay(gate_rows):
    running = jnp.cumsum(gate_rows, axis=0)
    block_total = running[-1]
    lag_matrix = running.T[:, :, None] - running.T[:, None, :]
    token_places = jnp.arange(gate_rows.shape[0])
    causal = (token_places[:, None] >= token_places[None, :])[None]
    decay_local = jnp.where(causal, jnp.exp(jnp.where(causal, lag_matrix, 0.0)), 0.0)
    return running, block_total, decay_local


def sequence_pass(seq_items, out_weight):
    queries, key_rows, value_rows, log_decay, out_grad = seq_items
    blocks = SEQUENCE_LENGTH // TOK_DEV
    scale_factor = 1.0 / DH
    block_shape = (blocks, TOK_DEV, HEAD_TOTAL, DH)
    query_blocks = queries.reshape(block_shape)
    key_blocks = key_rows.reshape(block_shape)
    value_blocks = value_rows.reshape(block_shape)
    gate_blocks = log_decay.reshape(blocks, TOK_DEV, HEAD_TOTAL)
    head_grad = jnp.dot(out_grad, out_weight.T, preferred_element_type=jnp.float32).astype(jnp.bfloat16)
    grad_blocks = head_grad.reshape(block_shape)

    def forward_step(state, inputs):
        query_rows, key_block, value_block, gate_rows = inputs
        running, block_total, decay_local = local_decay(gate_rows)
        query_float = query_rows.astype(jnp.float32)
        key_float = key_block.astype(jnp.float32)
        value_float = value_block.astype(jnp.float32)
        scores = jnp.einsum("thd,shd->hts", query_float, key_float, precision=HIGH)
        weights = (scores * decay_local * scale_factor).astype(jnp.bfloat16)
        weights_float = lax.optimization_barrier(weights).astype(jnp.float32)
        intra = jnp.einsum("hts,shd->thd", weights_float, value_float, precision=HIGH)
        growth = jnp.exp(running)[:, :, None]
        inter = jnp.einsum("thd,hde->the", query_float, state, precision=HIGH) * (growth * scale_factor)
        mixed = (intra + inter).astype(jnp.bfloat16)
        shrink = jnp.exp(block_total[None] - running)[:, :, None]
        fresh = jnp.einsum("thd,the->hde", key_float * shrink, value_float, precision=HIGH)
        return jnp.exp(block_total)[:, None, None] * state + fresh, (mixed, state)

    empty = jnp.zeros((HEAD_TOTAL, DH, DH), jnp.float32)
    final_state, (mixed_blocks, states_in) = lax.scan(forward_step, empty, (query_blocks, key_blocks, value_blocks, gate_blocks))
    mixed_all = mixed_blocks.reshape(SEQUENCE_LENGTH, HEAD_TOTAL * DH)
    projected = jnp.dot(mixed_all, out_weight, preferred_element_type=jnp.float32).astype(jnp.bfloat16)

    def backward_step(carry, inputs):
        query_rows, key_block, value_block, gate_rows, grad_rows, state = inputs
        running, block_total, decay_local = local_decay(gate_rows)
        query_float = query_rows.astype(jnp.float32)
        key_float = key_block.astype(jnp.float32)
        value_float = value_block.astype(jnp.float32)
        grad_float = grad_rows.astype(jnp.float32)
        growth = jnp.exp(running)[:, :, None]
        shrink = jnp.exp(block_total[None] - running)[:, :, None]
        scores = jnp.einsum("thd,shd->hts", query_float, key_float, precision=HIGH)
        weights = (scores * decay_local * scale_factor).astype(jnp.bfloat16)
        weights_float = lax.optimization_barrier(weights).astype(jnp.float32)
        grad_scores = jnp.einsum("the,she->hts", grad_float, value_float, precision=HIGH)
        grad_weights = (grad_scores * decay_local * scale_factor).astype(jnp.bfloat16)
        grad_weights_float = lax.optimization_barrier(grad_weights).astype(jnp.float32)
        query_grad = jnp.einsum("hts,shd->thd", grad_weights_float, key_float, precision=HIGH) + jnp.einsum("the,hde->thd", grad_float, state, precision=HIGH) * (growth * scale_factor)
        key_grad = jnp.einsum("hts,thd->shd", grad_weights_float, query_float, precision=HIGH) + jnp.einsum("hde,the->thd", carry, value_float, precision=HIGH) * (shrink * scale_factor)
        value_grad = jnp.einsum("hts,the->she", weights_float, grad_float, precision=HIGH) + jnp.einsum("hde,thd->the", carry, key_float, precision=HIGH) * (shrink * scale_factor)
        reach = jnp.einsum("thd,the->hde", query_float * growth, grad_float, precision=HIGH)
        new_carry = jnp.exp(block_total)[:, None, None] * carry + reach
        return new_carry, (query_grad.astype(jnp.bfloat16), key_grad.astype(jnp.bfloat16), value_grad.astype(jnp.bfloat16))

    first_carry, (query_grads, key_grads, value_grads) = lax.scan(backward_step, empty, (query_blocks, key_blocks, value_blocks, gate_blocks, grad_blocks, states_in), reverse=True)
    return (projected, query_grads.reshape(SEQUENCE_LENGTH, HEAD_TOTAL * DH), key_grads.reshape(SEQUENCE_LENGTH, HEAD_TOTAL * DH), value_grads.reshape(SEQUENCE_LENGTH, HEAD_TOTAL * DH))


def reference(queries, key_rows, value_rows, log_decay, out_weight, out_grad):
    results = lax.map(lambda seq_items: sequence_pass(seq_items, out_weight), (queries, key_rows, value_rows, log_decay, out_grad))
    return (results[0], results[1], results[2], results[3])
```

```python
import jax
import jax.numpy as jnp
from jax import lax
from jax.experimental import pallas as pl
from jax.experimental.pallas import tpu as pltpu
from jax.sharding import PartitionSpec as P

AXES = ("dp", "ctx")
F32 = jnp.float32
BF16 = jnp.bfloat16
HIGHEST = lax.Precision.HIGHEST
DH = 128
SCALE = 1.0 / DH
TOK = 128
SPAN = 2 * TOK
HEADS = 16
GROUP = 2
BAND = 4
STEPS = HEADS // GROUP
VMEM_LIMIT = 58 * 1024 * 1024


def device_place(x, y, z, core):
    return ((z % 4) * 4 + x) * 16 + y * 4 + (z // 4) * 2 + core


def moves(dx, dy, dz, dcore):
    pairs = []
    for x in range(4):
        for y in range(4):
            for z in range(8):
                for core in range(2):
                    target = ((x + dx) % 4, (y + dy) % 4, (z + dz) % 8, core ^ dcore)
                    pairs.append((device_place(x, y, z, core), device_place(*target)))
    return pairs


def shift(value, dx=0, dy=0, dz=0, dcore=0):
    return lax.ppermute(value, AXES, moves(dx, dy, dz, dcore))


def join_tokens(core, mine, other, axis=0):
    return jnp.where(
        core == 0,
        jnp.concatenate([mine, other], axis),
        jnp.concatenate([other, mine], axis),
    )


def dot(left, right, contract):
    return lax.dot_general(left, right, (contract, ((), ())), preferred_element_type=F32)


ROWS = ((0,), (0,))
PLAIN = ((1,), (0,))
COLS = ((1,), (1,))


def after(value, *others):
    return lax.optimization_barrier((value, *others))[0]


def split_kernel(place_ref, q_ref, k_ref, v_ref, mine_ref, other_ref):
    for h in range(HEADS):
        here = pl.ds(pl.multiple_of(place_ref[h], DH), DH)
        there = pl.ds(pl.multiple_of(place_ref[HEADS + h], DH), DH)
        for i, source in enumerate((q_ref, k_ref, v_ref)):
            mine_ref[i, :, columns(h)] = source[:, here]
            other_ref[i, :, columns(h)] = source[:, there]


def split_heads(place, arrays):
    return pl.pallas_call(
        split_kernel,
        in_specs=[SCALARS, *[WHOLE] * 3],
        out_specs=[WHOLE] * 2,
        out_shape=[shape(BF16, 3, TOK, HEADS * DH)] * 2,
        compiler_params=pltpu.CompilerParams(vmem_limit_bytes=VMEM_LIMIT),
        cost_estimate=pl.CostEstimate(flops=0, bytes_accessed=1 << 16, transcendentals=0),
    )(place, *arrays)


def merge_kernel(place_ref, dq_mine, both_mine, dq_other, both_other, *outs):
    mines = dq_mine.at[0], both_mine.at[0], both_mine.at[1]
    others = dq_other.at[0], both_other.at[0], both_other.at[1]
    for h in range(HEADS):
        here = pl.ds(pl.multiple_of(place_ref[h], DH), DH)
        there = pl.ds(pl.multiple_of(place_ref[HEADS + h], DH), DH)
        for mine, other, out in zip(mines, others, outs):
            out[:, here] = mine[:, columns(h)]
            out[:, there] = other[:, columns(h)]


def merge_heads(place, mine, other):
    return pl.pallas_call(
        merge_kernel,
        in_specs=[SCALARS, *[WHOLE] * 4],
        out_specs=[WHOLE] * 3,
        out_shape=[shape(BF16, TOK, 2 * HEADS * DH)] * 3,
        compiler_params=pltpu.CompilerParams(vmem_limit_bytes=VMEM_LIMIT),
        cost_estimate=pl.CostEstimate(flops=0, bytes_accessed=1 << 16, transcendentals=0),
    )(place, *mine, *other)


def columns(j):
    return slice(j * DH, (j + 1) * DH)


TOKENS = pl.BlockSpec((SPAN, GROUP * DH), lambda g: (0, g))
STATES = pl.BlockSpec((GROUP, DH, DH), lambda g: (g, 0, 0))
SQUARES = pl.BlockSpec((GROUP, SPAN, SPAN), lambda g: (g, 0, 0))
TALL = pl.BlockSpec((1, SPAN, GROUP), lambda g: (g, 0, 0))
WIDE = pl.BlockSpec((1, GROUP, SPAN), lambda g: (g, 0, 0))
PACKED = pl.BlockSpec((3, SPAN, GROUP * DH), lambda g: (0, 0, g))
HALVES = pl.BlockSpec((2, TOK, GROUP * DH), lambda g: (0, 0, g))
HALF = pl.BlockSpec((1, TOK, GROUP * DH), lambda g: (0, 0, g))
SLAB = pl.BlockSpec((1, DH, DH), lambda g: (HEADS, 0, 0))
WHOLE = pl.BlockSpec(memory_space=pltpu.VMEM)
SCALARS = pl.BlockSpec(memory_space=pltpu.SMEM)
UNREAD = pl.BlockSpec(memory_space=pl.ANY)


def shape(dtype, *dims):
    return jax.ShapeDtypeStruct(dims, dtype)


def per_heads(kernel, ins, specs, outs, out_specs, flops, scratch=(), grid=(STEPS,)):
    return pl.pallas_call(
        kernel,
        grid=grid,
        in_specs=specs,
        out_specs=out_specs,
        out_shape=outs,
        scratch_shapes=scratch,
        compiler_params=pltpu.CompilerParams(vmem_limit_bytes=VMEM_LIMIT),
        cost_estimate=pl.CostEstimate(flops=flops // 64, bytes_accessed=1 << 16, transcendentals=0),
    )(*ins)


def split_rows(value):
    high = value.astype(BF16)
    rest = value - high.astype(F32)
    middle = rest.astype(BF16)
    return high, middle, (rest - middle.astype(F32)).astype(BF16)


def put_sums(message_ref, sums):
    message_ref[HEADS] = jnp.zeros((DH, DH), BF16)
    for i, part in enumerate(split_rows(sums)):
        message_ref[HEADS, i * HEADS : (i + 1) * HEADS, :] = part


def sums_of(slab):
    rows = [slab[i * HEADS : (i + 1) * HEADS, :].astype(F32) for i in range(3)]
    return rows[0] + rows[1] + rows[2]


def fresh_kernel(k_ref, v_ref, tall_ref, sums_ref, fresh_ref):
    for h in range(HEADS):
        run = tall_ref[h // GROUP, :, h % GROUP : h % GROUP + 1]
        shrink = jnp.exp(run[SPAN - 1 :] - run)
        keys = (k_ref[0, :, columns(h)].astype(F32) * shrink).astype(BF16)
        fresh_ref[h] = dot(keys, v_ref[0, :, columns(h)], ROWS).astype(BF16)
    put_sums(fresh_ref, sums_ref[...])


def weights_kernel(qkv_ref, tall_ref, wide_ref, decay_ref, weights_ref):
    later = lax.broadcasted_iota(jnp.int32, (SPAN, SPAN), 0)
    earlier = lax.broadcasted_iota(jnp.int32, (SPAN, SPAN), 1)
    causal = later >= earlier
    for j in range(GROUP):
        lag = tall_ref[0, :, j : j + 1] - wide_ref[0, j : j + 1, :]
        decay = jnp.where(causal, jnp.exp(jnp.where(causal, lag, 0.0)), 0.0) * SCALE
        decay_ref[j] = decay
        scores = dot(qkv_ref[0, :, columns(j)], qkv_ref[1, :, columns(j)], COLS)
        weights_ref[j] = (scores * decay).astype(BF16)


def pair_kernel(flags_ref, mine_ref, theirs_ref, pair_ref):
    ours, others = sums_of(mine_ref[HEADS]), sums_of(theirs_ref[HEADS])
    decays_mine = flags_ref[0] == 1.0
    mine_factor = jnp.where(decays_mine, jnp.exp(others), 1.0)
    theirs_factor = jnp.where(decays_mine, 1.0, jnp.exp(ours))
    for h in range(HEADS):
        mine = mine_ref[h].astype(F32) * mine_factor[h : h + 1]
        theirs = theirs_ref[h].astype(F32) * theirs_factor[h : h + 1]
        pair_ref[h] = (mine + theirs).astype(BF16)
    put_sums(pair_ref, ours + others)


def carried(flags_ref, head, j, theirs, one, two, three):
    wanted = lax.broadcasted_iota(jnp.int32, (HEADS, DH), 0) == head

    def row(slab_ref):
        return jnp.sum(jnp.where(wanted, sums_of(slab_ref[0]), 0.0), axis=0, keepdims=True)

    (theirs_ref, theirs_slab), (one_ref, one_slab), (two_ref, two_slab) = theirs, one, two
    first, second = row(one_slab), row(two_slab)
    at_end = flags_ref[4] == 1.0
    last = jnp.where(at_end, 1.0, jnp.exp(row(theirs_slab)))
    total = one_ref[j].astype(F32) * flags_ref[1]
    total += two_ref[j].astype(F32) * (jnp.exp(first) * flags_ref[2])
    total += three[j].astype(F32) * (jnp.exp(first + second) * flags_ref[3])
    total = total * last + theirs_ref[j].astype(F32) * jnp.where(at_end, 0.0, 1.0)
    return total.astype(BF16)


CARRIED = [STATES, SLAB] * 3 + [STATES]


def carried_operands(received):
    theirs, one, two, three = received
    return theirs, theirs, one, one, two, two, three


def carried_refs(refs):
    return (refs[0], refs[1]), (refs[2], refs[3]), (refs[4], refs[5]), refs[6]


def mixed_kernel(flags_ref, *refs):
    weights_ref, qkv_ref, tall_ref, _, mixed_ref, state_ref = refs[7:]
    for j in range(GROUP):
        head = pl.program_id(0) * GROUP + j
        state = carried(flags_ref, head, j, *carried_refs(refs))
        state_ref[j] = state
        growth = jnp.exp(tall_ref[0, :, j : j + 1]) * SCALE
        intra = dot(weights_ref[j], qkv_ref[2, :, columns(j)], PLAIN)
        inter = dot(qkv_ref[0, :, columns(j)], state, PLAIN) * growth
        mixed_ref[:, columns(j)] = (intra + inter).astype(BF16)


def head_grad_kernel(og_ref, w0, w1, w2, w3, q_ref, tall_ref, _grads, _reach, *refs):
    *blocks, grad_ref, reach_ref = refs
    wide, quarter = blocks[0].shape[2], w0.shape[1]
    row = 0
    for block in blocks:
        count = block.shape[0]
        rows = slice(row * DH, (row + count) * DH)
        total = dot(block[...].reshape(count * DH, wide), og_ref[:wide], PLAIN)
        for i, part in enumerate((w0, w1, w2, w3)):
            at = wide + i * quarter
            total += dot(part[rows], og_ref[at : at + quarter], PLAIN)
        for i in range(count):
            j = row + i
            grads = total[columns(i)].T.astype(BF16)
            grad_ref[:, columns(j)] = grads
            growth = jnp.exp(tall_ref[j // GROUP, :, j % GROUP : j % GROUP + 1])
            queries = (q_ref[0, :, columns(j)].astype(F32) * growth).astype(BF16)
            reach_ref[j] = dot(queries, grads, ROWS).astype(BF16)
        row += count


def band_grads(band, og, blocks, weight_y, qkv, tall, grads, reach):
    quarter = weight_y[0].shape[1]
    rows = BAND * DH
    here = pl.BlockSpec((rows, quarter), lambda g: (band, 0))
    over = pl.BlockSpec((rows, quarter), lambda g: (band % 2, 0))

    def full(value):
        return pl.BlockSpec(value.shape, lambda g: (0,) * value.ndim)

    if grads is None:
        aliases, grads_in = {8: 1}, tall
    else:
        aliases, grads_in = {7: 0, 8: 1}, grads
    return pl.pallas_call(
        head_grad_kernel,
        grid=(1,),
        in_specs=[
            full(og), here, here, here, over,
            pl.BlockSpec((1, SPAN, rows), lambda g: (0, 0, band)),
            pl.BlockSpec((BAND // GROUP, SPAN, GROUP), lambda g: (band, 0, 0)),
            UNREAD, UNREAD, *[full(block) for block in blocks],
        ],
        out_specs=[
            pl.BlockSpec((SPAN, rows), lambda g: (0, band)),
            pl.BlockSpec((BAND, DH, DH), lambda g: (band, 0, 0)),
        ],
        out_shape=[shape(BF16, SPAN, HEADS * DH), shape(BF16, HEADS + 1, DH, DH)],
        input_output_aliases=aliases,
        compiler_params=pltpu.CompilerParams(vmem_limit_bytes=VMEM_LIMIT),
        cost_estimate=pl.CostEstimate(flops=1 << 24, bytes_accessed=1 << 16, transcendentals=0),
    )(og, *weight_y[:3], weight_y[3 + band // 2], qkv, tall, grads_in, reach, *blocks)


def local_grad_kernel(
    core_ref, grad_ref, qkv_ref, state_ref, weights_ref, decay_ref, tall_ref,
    mine_ref, send_ref, dk_ref, dv_ref, dq_ref,
):
    core = core_ref[0]
    for j in range(GROUP):
        at = columns(j)
        grads = grad_ref[:, at]
        growth = jnp.exp(tall_ref[0, :, j : j + 1]) * SCALE
        scores = dot(grads, qkv_ref[2, :, at], COLS)
        grad_weights = (scores * decay_ref[j]).astype(BF16)
        rest = dot(grads, state_ref[j], COLS) * growth
        dq_ref[:, at] = (dot(grad_weights, qkv_ref[1, :, at], PLAIN) + rest).astype(BF16)
        dk_ref[:, at] = dot(grad_weights, qkv_ref[0, :, at], ROWS)
        dv_ref[:, at] = dot(weights_ref[j], grads, ROWS)
    mine_ref[0] = dq_ref[pl.ds(pl.multiple_of(core * TOK, TOK), TOK), :]
    send_ref[0] = dq_ref[pl.ds(pl.multiple_of((1 - core) * TOK, TOK), TOK), :]


def carried_grad_kernel(core_ref, flags_ref, *refs):
    dk_in, dv_in, qkv_ref, tall_ref, _, _unread, mine_ref, send_ref, both_ref = refs[7:]
    core = core_ref[0]
    for j in range(GROUP):
        at = columns(j)
        head = pl.program_id(0) * GROUP + j
        state = carried(flags_ref, head, j, *carried_refs(refs))
        run = tall_ref[0, :, j : j + 1]
        shrink = jnp.exp(run[SPAN - 1 :] - run) * SCALE
        keys = dk_in[:, at] + dot(qkv_ref[2, :, at], state, COLS) * shrink
        values = dv_in[:, at] + dot(qkv_ref[1, :, at], state, PLAIN) * shrink
        both_ref[0, :, at] = keys.astype(BF16)
        both_ref[1, :, at] = values.astype(BF16)
    for i in range(2):
        mine_ref[i] = both_ref[i, pl.ds(pl.multiple_of(core * TOK, TOK), TOK), :]
        send_ref[i] = both_ref[i, pl.ds(pl.multiple_of((1 - core) * TOK, TOK), TOK), :]


def project_kernel(place_ref, mixed_ref, *refs):
    core, y = place_ref[0], place_ref[1]
    blocks, quarters = refs[:5], refs[5:10]
    mine_x, send_x, mine_y, send_y, part_ref = refs[10:]
    mixed = mixed_ref[...]
    wide, quarter = blocks[0].shape[2], quarters[0].shape[1]
    middle = quarters[3].shape[0]

    def put(value, mine_ref, send_ref, at):
        part_ref[...] = value
        at = pl.multiple_of(at, DH)
        mine_ref[:, pl.ds(at, quarter)] = part_ref[pl.ds(pl.multiple_of(core * TOK, TOK), TOK), :]
        send = part_ref[pl.ds(pl.multiple_of((1 - core) * TOK, TOK), TOK), :]
        send_ref[:, pl.ds(at, quarter)] = send.astype(BF16)

    for i in range(wide // quarter):
        total = jnp.zeros((SPAN, quarter), F32)
        row = 0
        for block in blocks:
            part = block[:, :, i * quarter : (i + 1) * quarter].reshape(-1, quarter)
            total += dot(mixed[:, row : row + part.shape[0]], part, PLAIN)
            row += part.shape[0]
        put(total, mine_x, send_x, i * quarter)
    for step, part in ((0, quarters[0]), (3, quarters[1]), (1, quarters[2])):
        put(dot(mixed, part[...], PLAIN), mine_y, send_y, (y + step) % 4 * quarter)
    far = dot(mixed[:, :middle], quarters[3][...], PLAIN)
    far += dot(mixed[:, middle:], quarters[4][...], PLAIN)
    put(far, mine_y, send_y, (y + 2) % 4 * quarter)


def through_chips(state, theirs, flags, direction):
    pair = pl.pallas_call(
        pair_kernel,
        in_specs=[SCALARS, WHOLE, WHOLE],
        out_specs=WHOLE,
        out_shape=shape(BF16, HEADS + 1, DH, DH),
        compiler_params=pltpu.CompilerParams(vmem_limit_bytes=VMEM_LIMIT),
        cost_estimate=pl.CostEstimate(flops=0, bytes_accessed=1 << 16, transcendentals=0),
    )(flags, state, theirs)
    ring = shift(pair, dy=direction), shift(pair, dy=2), shift(pair, dy=-direction)
    return (theirs, *ring), pair


def shards(queries, key_rows, value_rows, log_decay, out_weight, out_grad):
    dp, ctx = lax.axis_index("dp"), lax.axis_index("ctx")
    z_low, x = dp // 4, dp % 4
    y, z_high, core = ctx // 4, (ctx // 2) % 2, ctx % 2
    width = out_weight.shape[1]
    wide, quarter = width // 2, width // 8

    steps = jnp.array([0, 3, 1, 2], jnp.int32)
    order = ((z_low + steps[None, :]) % 4 * 4 + (x + steps[:, None]) % 4).reshape(HEADS)
    heads = jnp.concatenate([2 * order + core, 2 * order + 1 - core]).astype(jnp.int32)
    place = heads * DH

    rows = lax.dynamic_slice_in_dim(out_weight, core * TOK, TOK, 0)
    part = lax.dynamic_slice_in_dim(rows, wide + y * quarter, quarter, 1)
    near = jnp.concatenate([part, shift(part, dz=1), shift(part, dz=-1), shift(part, dz=2)], 0)
    mine, other = split_heads(place, (queries[0], key_rows[0], value_rows[0]))
    near = after(near, other)
    plane = jnp.concatenate([near, shift(near, dx=1), shift(near, dx=-1), shift(near, dx=2)], 0)
    part = after(rows[:, :wide], near)
    column = jnp.stack([part, shift(part, dz=1), shift(part, dz=-1), shift(part, dz=2)])

    plane = after(plane, column)
    y_before, y_behind = shift(plane, dy=1), shift(plane, dy=-1)

    qkv = join_tokens(core, mine, shift(after(other, plane), dcore=1), 1)
    grad_rows = join_tokens(core, out_grad[0], shift(after(out_grad[0], plane), dcore=1))
    quarters = [
        lax.dynamic_slice_in_dim(grad_rows, wide + (y + step) % 4 * quarter, quarter, 1)
        for step in (0, 3, 1, 2)
    ]
    grad_columns = jnp.concatenate([grad_rows[:, :wide], *quarters], 1).T

    pick = (jnp.arange(2 * HEADS)[:, None] == heads[None, :]).astype(F32)
    gates = jnp.dot(log_decay[0], pick, precision=HIGHEST)
    gates = join_tokens(
        core, gates[:, :HEADS], shift(after(gates[:, HEADS:], plane), dcore=1)
    )
    places = jnp.arange(SPAN)
    lower = (places[:, None] >= places[None, :]).astype(F32)
    running = jnp.dot(lower, gates, precision=HIGHEST)
    wide_run = running.T.reshape(STEPS, GROUP, SPAN)
    tall_run = wide_run.transpose(0, 2, 1)
    sums = jnp.broadcast_to(running[SPAN - 1][:, None], (HEADS, DH))
    forward = jnp.stack([z_high == 0, y >= 1, y >= 2, y >= 3, z_high == 0]).astype(F32)
    backward = jnp.stack([z_high == 1, y <= 2, y <= 1, y <= 0, z_high == 1]).astype(F32)

    decay, weights = per_heads(
        weights_kernel,
        (qkv, tall_run, wide_run),
        [PACKED, TALL, WIDE],
        [shape(F32, HEADS, SPAN, SPAN), shape(BF16, HEADS, SPAN, SPAN)],
        [SQUARES, SQUARES],
        2 * HEADS * SPAN * SPAN * DH,
    )
    fresh = per_heads(
        fresh_kernel,
        (qkv, qkv, tall_run, sums),
        [
            pl.BlockSpec((1, SPAN, HEADS * DH), lambda g: (1, 0, 0)),
            pl.BlockSpec((1, SPAN, HEADS * DH), lambda g: (2, 0, 0)),
            pl.BlockSpec((STEPS, SPAN, GROUP), lambda g: (0, 0, 0)),
            pl.BlockSpec((HEADS, DH), lambda g: (0, 0)),
        ],
        shape(BF16, HEADS + 1, DH, DH),
        pl.BlockSpec((HEADS + 1, DH, DH), lambda g: (0, 0, 0)),
        2 * HEADS * SPAN * DH * DH,
        grid=(1,),
    )

    middle = plane.shape[0] // 2
    halves = after((y_before[:middle], y_behind[middle:]), fresh, weights)
    weight_y = [
        plane, y_before, y_behind, shift(halves[0], dy=1), shift(halves[1], dy=-1)
    ]
    before, behind = shift(column, dx=1), shift(column, dx=-1)
    first, second = shift(before[:2], dx=1), shift(behind[2:], dx=-1)
    bands = [(column,), (before,), (behind,), (first, second)]
    theirs = shift(fresh, dz=4)
    received, _ = through_chips(fresh, after(theirs, *weight_y[3:]), forward, 1)

    grads, reach = None, after(fresh, theirs)
    for band, blocks in enumerate(bands):
        grads, reach = band_grads(
            band, grad_columns, blocks, weight_y, qkv, tall_run, grads, reach
        )
    theirs = shift(reach, dz=4)
    mixed, incoming = per_heads(
        mixed_kernel,
        (forward, *carried_operands(received), weights, qkv, tall_run, reach),
        [SCALARS, *CARRIED, SQUARES, PACKED, TALL, UNREAD],
        [shape(BF16, SPAN, HEADS * DH), shape(BF16, HEADS, DH, DH)],
        [TOKENS, STATES],
        2 * HEADS * SPAN * (SPAN + DH) * DH,
    )
    returned, pair = through_chips(reach, after(theirs, incoming), backward, -1)
    dq_mine, dq_send, dk, dv = per_heads(
        local_grad_kernel,
        (core[None], after(grads, pair), qkv, incoming, weights, decay, tall_run),
        [SCALARS, TOKENS, PACKED, STATES, SQUARES, SQUARES, TALL],
        [
            *[shape(BF16, 1, TOK, HEADS * DH)] * 2,
            *[shape(F32, SPAN, HEADS * DH)] * 2,
        ],
        [HALF, HALF, TOKENS, TOKENS],
        2 * HEADS * SPAN * DH * (4 * SPAN + DH),
        [pltpu.VMEM((SPAN, GROUP * DH), BF16)],
    )

    mine_x, send_x, mine_y, send_y = pl.pallas_call(
        project_kernel,
        in_specs=[SCALARS, *[WHOLE] * 11],
        out_specs=[WHOLE] * 4,
        out_shape=[
            shape(F32, TOK, wide), shape(BF16, TOK, wide),
            shape(F32, TOK, wide), shape(BF16, TOK, wide),
        ],
        scratch_shapes=[pltpu.VMEM((SPAN, quarter), F32)],
        compiler_params=pltpu.CompilerParams(vmem_limit_bytes=VMEM_LIMIT),
        cost_estimate=pl.CostEstimate(flops=1 << 24, bytes_accessed=1 << 16, transcendentals=0),
    )(
        jnp.stack([core, y]),
        after(mixed, pair),
        *[block for blocks in bands for block in blocks],
        *weight_y,
    )
    mine, send = per_heads(
        carried_grad_kernel,
        (
            core[None], backward, *carried_operands(returned), dk, dv, qkv, tall_run,
            send_y, dq_send,
        ),
        [SCALARS, SCALARS, *CARRIED, TOKENS, TOKENS, PACKED, TALL, UNREAD, UNREAD],
        [shape(BF16, 2, TOK, HEADS * DH)] * 2,
        [HALVES] * 2,
        4 * HEADS * SPAN * DH * DH,
        [pltpu.VMEM((2, SPAN, GROUP * DH), BF16)],
    )
    query_grad, key_grad, value_grad = merge_heads(
        place,
        (dq_mine, mine),
        (shift(after(dq_send, mine), dcore=1), shift(send, dcore=1)),
    )
    projected = jnp.concatenate(
        [
            mine_x + shift(after(send_x, mine), dcore=1).astype(F32),
            mine_y + shift(after(send_y, mine), dcore=1).astype(F32),
        ],
        1,
    ).astype(BF16)
    return projected[None], query_grad[None], key_grad[None], value_grad[None]


def solution(mesh):
    tokens = P("dp", "ctx", None)
    return jax.shard_map(
        shards,
        mesh=mesh,
        in_specs=(tokens, tokens, tokens, tokens, P("dp", None), tokens),
        out_specs=(tokens,) * 4,
        check_vma=False,
    )
```

```python
import jax
import jax.numpy as jnp
from jax import lax
from jax.experimental import pallas as pl
from jax.experimental.pallas import tpu as pltpu
from jax.sharding import PartitionSpec as P

AXES = ("dp", "ctx")
F32 = jnp.float32
BF16 = jnp.bfloat16
HIGHEST = lax.Precision.HIGHEST
DH = 128
SCALE = 1.0 / DH
TOK = 128
SPAN = 2 * TOK
HEADS = 16
GROUP = 2
HALF_HEADS = HEADS // 2
BAND = 4
STEPS = HEADS // GROUP
VMEM_LIMIT = 58 * 1024 * 1024


def device_place(x, y, z, core):
    return ((z % 4) * 4 + x) * 16 + y * 4 + (z // 4) * 2 + core


def moves(dx, dy, dz, dcore):
    pairs = []
    for x in range(4):
        for y in range(4):
            for z in range(8):
                for core in range(2):
                    target = ((x + dx) % 4, (y + dy) % 4, (z + dz) % 8, core ^ dcore)
                    pairs.append((device_place(x, y, z, core), device_place(*target)))
    return pairs


def shift(value, dx=0, dy=0, dz=0, dcore=0):
    return lax.ppermute(value, AXES, moves(dx, dy, dz, dcore))


def join_tokens(core, mine, other, axis=0):
    return jnp.where(
        core == 0,
        jnp.concatenate([mine, other], axis),
        jnp.concatenate([other, mine], axis),
    )


def dot(left, right, contract):
    return lax.dot_general(left, right, (contract, ((), ())), preferred_element_type=F32)


ROWS = ((0,), (0,))
PLAIN = ((1,), (0,))
COLS = ((1,), (1,))


def after(value, *others):
    return lax.optimization_barrier((value, *others))[0]


def split_kernel(place_ref, q_ref, k_ref, v_ref, mine_ref, other_ref):
    for h in range(HEADS):
        here = pl.ds(pl.multiple_of(place_ref[h], DH), DH)
        there = pl.ds(pl.multiple_of(place_ref[HEADS + h], DH), DH)
        for i, source in enumerate((q_ref, k_ref, v_ref)):
            mine_ref[i, :, columns(h)] = source[:, here]
            other_ref[i, :, columns(h)] = source[:, there]


def split_heads(place, arrays):
    return pl.pallas_call(
        split_kernel,
        in_specs=[SCALARS, *[WHOLE] * 3],
        out_specs=[WHOLE] * 2,
        out_shape=[shape(BF16, 3, TOK, HEADS * DH)] * 2,
        compiler_params=pltpu.CompilerParams(vmem_limit_bytes=VMEM_LIMIT),
        cost_estimate=pl.CostEstimate(flops=0, bytes_accessed=1 << 16, transcendentals=0),
    )(place, *arrays)


def merge_kernel(place_ref, *refs):
    mines, others, outs = refs[:3], refs[3:6], refs[6:]
    for h in range(HEADS):
        here = pl.ds(pl.multiple_of(place_ref[h], DH), DH)
        there = pl.ds(pl.multiple_of(place_ref[HEADS + h], DH), DH)
        half = columns(h % HALF_HEADS)
        for sources, at in ((mines, here), (others, there)):
            outs[0][:, at] = sources[0][0, :, columns(h)]
            for i in range(2):
                outs[1 + i][:, at] = sources[1 + h // HALF_HEADS][i, :, half]


def merge_heads(place, mines, others):
    return pl.pallas_call(
        merge_kernel,
        in_specs=[SCALARS, *[WHOLE] * 6],
        out_specs=[WHOLE] * 3,
        out_shape=[shape(BF16, TOK, 2 * HEADS * DH)] * 3,
        compiler_params=pltpu.CompilerParams(vmem_limit_bytes=VMEM_LIMIT),
        cost_estimate=pl.CostEstimate(flops=0, bytes_accessed=1 << 16, transcendentals=0),
    )(place, *mines, *others)


def columns(j):
    return slice(j * DH, (j + 1) * DH)


TOKENS = pl.BlockSpec((SPAN, GROUP * DH), lambda g: (0, g))
STATES = pl.BlockSpec((GROUP, DH, DH), lambda g: (g, 0, 0))
SQUARES = pl.BlockSpec((GROUP, SPAN, SPAN), lambda g: (g, 0, 0))
TALL = pl.BlockSpec((1, SPAN, GROUP), lambda g: (g, 0, 0))
WIDE = pl.BlockSpec((1, GROUP, SPAN), lambda g: (g, 0, 0))
PACKED = pl.BlockSpec((3, SPAN, GROUP * DH), lambda g: (0, 0, g))
HALVES = pl.BlockSpec((2, TOK, GROUP * DH), lambda g: (0, 0, g))
HALF = pl.BlockSpec((1, TOK, GROUP * DH), lambda g: (0, 0, g))
SLAB = pl.BlockSpec((1, DH, DH), lambda g: (HEADS, 0, 0))
WHOLE = pl.BlockSpec(memory_space=pltpu.VMEM)
SCALARS = pl.BlockSpec(memory_space=pltpu.SMEM)
UNREAD = pl.BlockSpec(memory_space=pl.ANY)


def shape(dtype, *dims):
    return jax.ShapeDtypeStruct(dims, dtype)


def per_heads(kernel, ins, specs, outs, out_specs, flops, scratch=(), grid=(STEPS,)):
    return pl.pallas_call(
        kernel,
        grid=grid,
        in_specs=specs,
        out_specs=out_specs,
        out_shape=outs,
        scratch_shapes=scratch,
        compiler_params=pltpu.CompilerParams(vmem_limit_bytes=VMEM_LIMIT),
        cost_estimate=pl.CostEstimate(flops=flops // 64, bytes_accessed=1 << 16, transcendentals=0),
    )(*ins)


def split_rows(value):
    high = value.astype(BF16)
    rest = value - high.astype(F32)
    middle = rest.astype(BF16)
    return high, middle, (rest - middle.astype(F32)).astype(BF16)


def put_sums(message_ref, *sums):
    message_ref[HEADS] = jnp.zeros((DH, DH), BF16)
    parts = [part for rows in sums for part in split_rows(rows)]
    for i, part in enumerate(parts):
        message_ref[HEADS, i * HEADS : (i + 1) * HEADS, :] = part


def sums_of(slab, which=0):
    starts = [(3 * which + i) * HEADS for i in range(3)]
    rows = [slab[start : start + HEADS, :].astype(F32) for start in starts]
    return rows[0] + rows[1] + rows[2]


def fresh_kernel(k_ref, v_ref, tall_ref, sums_ref, fresh_ref):
    for h in range(HEADS):
        run = tall_ref[h // GROUP, :, h % GROUP : h % GROUP + 1]
        shrink = jnp.exp(run[SPAN - 1 :] - run)
        keys = (k_ref[0, :, columns(h)].astype(F32) * shrink).astype(BF16)
        fresh_ref[h] = dot(keys, v_ref[0, :, columns(h)], ROWS).astype(BF16)
    put_sums(fresh_ref, sums_ref[...])


def weights_kernel(qkv_ref, tall_ref, wide_ref, decay_ref, weights_ref):
    later = lax.broadcasted_iota(jnp.int32, (SPAN, SPAN), 0)
    earlier = lax.broadcasted_iota(jnp.int32, (SPAN, SPAN), 1)
    causal = later >= earlier
    for j in range(GROUP):
        lag = tall_ref[0, :, j : j + 1] - wide_ref[0, j : j + 1, :]
        decay = jnp.where(causal, jnp.exp(jnp.where(causal, lag, 0.0)), 0.0) * SCALE
        decay_ref[j] = decay
        scores = dot(qkv_ref[0, :, columns(j)], qkv_ref[1, :, columns(j)], COLS)
        weights_ref[j] = (scores * decay).astype(BF16)


def pair_kernel(flags_ref, mine_ref, theirs_ref, pair_ref):
    ours, others = sums_of(mine_ref[HEADS]), sums_of(theirs_ref[HEADS])
    decays_mine = flags_ref[0] == 1.0
    mine_factor = jnp.where(decays_mine, jnp.exp(others), 1.0)
    theirs_factor = jnp.where(decays_mine, 1.0, jnp.exp(ours))
    for h in range(HEADS):
        mine = mine_ref[h].astype(F32) * mine_factor[h : h + 1]
        theirs = theirs_ref[h].astype(F32) * theirs_factor[h : h + 1]
        pair_ref[h] = (mine + theirs).astype(BF16)
    put_sums(
        pair_ref,
        jnp.where(decays_mine, ours, others),
        jnp.where(decays_mine, others, ours),
    )


def carried(flags_ref, head, j, theirs, one, two, three):
    wanted = lax.broadcasted_iota(jnp.int32, (HEADS, DH), 0) == head

    def row(slab_ref, count=1):
        sums = sum(sums_of(slab_ref[0], i) for i in range(count))
        return jnp.sum(jnp.where(wanted, sums, 0.0), axis=0, keepdims=True)

    (theirs_ref, theirs_slab), (one_ref, one_slab), (two_ref, two_slab) = theirs, one, two
    first, second = row(one_slab, 2), row(two_slab, 2)
    at_end = flags_ref[4] == 1.0
    last = jnp.where(at_end, 1.0, jnp.exp(row(theirs_slab)))
    total = one_ref[j].astype(F32) * flags_ref[1]
    total += two_ref[j].astype(F32) * (jnp.exp(first) * flags_ref[2])
    total += three[j].astype(F32) * (jnp.exp(first + second) * flags_ref[3])
    total = total * last + theirs_ref[j].astype(F32) * jnp.where(at_end, 0.0, 1.0)
    return total.astype(BF16)


CARRIED = [STATES, SLAB] * 3 + [STATES]


def carried_operands(received):
    theirs, one, two, three = received
    return theirs, theirs, one, one, two, two, three


def carried_refs(refs):
    return (refs[0], refs[1]), (refs[2], refs[3]), (refs[4], refs[5]), refs[6]


def mixed_kernel(flags_ref, *refs):
    weights_ref, qkv_ref, tall_ref, _, mixed_ref, state_ref = refs[7:]
    for j in range(GROUP):
        head = pl.program_id(0) * GROUP + j
        state = carried(flags_ref, head, j, *carried_refs(refs))
        state_ref[j] = state
        growth = jnp.exp(tall_ref[0, :, j : j + 1]) * SCALE
        intra = dot(weights_ref[j], qkv_ref[2, :, columns(j)], PLAIN)
        inter = dot(qkv_ref[0, :, columns(j)], state, PLAIN) * growth
        mixed_ref[:, columns(j)] = (intra + inter).astype(BF16)


def head_grad_kernel(og_ref, q_ref, tall_ref, *refs):
    blocks, quarters = refs[:5], refs[5:10]
    grad_ref, *reach_refs, wx_ref, wy_ref, sems = refs[10:]
    wide, quarter = wx_ref.shape[2], wy_ref.shape[2]
    size = BAND * DH

    def copies(band):
        if band < 3:
            pairs = [(blocks[band], wx_ref.at[band * BAND : (band + 1) * BAND])]
        else:
            half = BAND // 2
            starts = band * BAND, band * BAND + half
            pairs = [
                (block, wx_ref.at[start : start + half])
                for block, start in zip(blocks[3:], starts)
            ]
        rows = slice(band * size, (band + 1) * size)
        over = slice(band % 2 * size, (band % 2 + 1) * size)
        for i in range(3):
            pairs.append((quarters[i].at[rows], wy_ref.at[i, rows]))
        pairs.append((quarters[3 + band // 2].at[over], wy_ref.at[3, rows]))
        return [
            pltpu.make_async_copy(source, target, sems.at[band, i])
            for i, (source, target) in enumerate(pairs)
        ]

    bands = [copies(band) for band in range(HEADS // BAND)]
    for band in bands:
        for copy in band:
            copy.start()
    for band, waited in enumerate(bands):
        for copy in waited:
            copy.wait()
        rows = slice(band * size, (band + 1) * size)
        block = wx_ref[band * BAND : (band + 1) * BAND].reshape(size, wide)
        total = dot(block, og_ref[:wide], PLAIN)
        for i in range(4):
            at = wide + i * quarter
            total += dot(wy_ref[i, rows], og_ref[at : at + quarter], PLAIN)
        for i in range(BAND):
            head = band * BAND + i
            grads = total[columns(i)].T.astype(BF16)
            grad_ref[:, columns(head)] = grads
            run = tall_ref[head // GROUP, :, head % GROUP : head % GROUP + 1]
            queries = (q_ref[0, :, columns(head)].astype(F32) * jnp.exp(run)).astype(BF16)
            reach = dot(queries, grads, ROWS).astype(BF16)
            reach_refs[head // HALF_HEADS][head % HALF_HEADS] = reach


def head_grads(og, blocks, weight_y, qkv, tall):
    wide, quarter = blocks[0].shape[2], weight_y[0].shape[1]
    return pl.pallas_call(
        head_grad_kernel,
        grid=(1,),
        in_specs=[
            pl.BlockSpec(og.shape, lambda g: (0, 0)),
            pl.BlockSpec((1, SPAN, HEADS * DH), lambda g: (0, 0, 0)),
            pl.BlockSpec(tall.shape, lambda g: (0, 0, 0)),
            *[UNREAD] * 10,
        ],
        out_specs=[
            pl.BlockSpec((SPAN, HEADS * DH), lambda g: (0, 0)),
            *[pl.BlockSpec((HALF_HEADS, DH, DH), lambda g: (0, 0, 0))] * 2,
        ],
        out_shape=[
            shape(BF16, SPAN, HEADS * DH),
            *[shape(BF16, HALF_HEADS, DH, DH)] * 2,
        ],
        scratch_shapes=[
            pltpu.VMEM((HEADS, DH, wide), BF16),
            pltpu.VMEM((4, HEADS * DH, quarter), BF16),
            pltpu.SemaphoreType.DMA((HEADS // BAND, 6)),
        ],
        compiler_params=pltpu.CompilerParams(vmem_limit_bytes=VMEM_LIMIT),
        cost_estimate=pl.CostEstimate(flops=1 << 24, bytes_accessed=1 << 16, transcendentals=0),
    )(og, qkv, tall, *blocks, *weight_y)


def table_kernel(flags_ref, own_ref, theirs_ref, one_ref, two_ref, three_ref, table_ref):
    at_start = flags_ref[0] == 1.0
    own, other = sums_of(own_ref[0]), sums_of(theirs_ref[0])
    inner = [sums_of(ref[0], 0) for ref in (three_ref, two_ref, one_ref)]
    pairs = [rest + sums_of(ref[0], 1) for rest, ref in zip(inner, (three_ref, two_ref, one_ref))]
    valid = [flags_ref[i] for i in (1, 2, 3)]
    beyond = [jnp.zeros_like(own), pairs[0], pairs[0] + pairs[1]]
    zero, one = jnp.zeros_like(own), jnp.ones_like(own)
    last = jnp.where(at_start, one, jnp.exp(other))

    plain = [v * jnp.exp(log_sum) for v, log_sum in zip(valid, beyond)]
    first = [part * last for part in plain] + [jnp.where(at_start, zero, one)]
    first += [jnp.where(at_start, jnp.exp(other), one), jnp.where(at_start, one, jnp.exp(own))]

    through = [v * jnp.exp(log_sum + rest) for v, log_sum, rest in zip(valid, beyond, inner)]
    ring = [jnp.where(at_start, a, b) for a, b in zip(through, plain)]
    second = [part * last for part in ring] + [one, jnp.where(at_start, one, zero)]
    second += [part * jnp.where(at_start, jnp.exp(own), one) for part in ring]
    for h in range(HEADS):
        for i, rows in enumerate(first if h < HALF_HEADS else second):
            table_ref[h, i : i + 1, :] = rows[h : h + 1]


def weighted(table, first_row, *parts):
    total = None
    for i, part in enumerate(parts):
        term = part.astype(F32) * table[first_row + i : first_row + i + 1]
        total = term if total is None else total + term
    return total.astype(BF16)


def between_kernel(table_ref, *refs):
    *parts, out_ref = refs
    for h in range(HALF_HEADS):
        out_ref[h] = weighted(table_ref[h], 4, *[part[h] for part in parts])


def between(table, half, *parts):
    return pl.pallas_call(
        between_kernel,
        grid=(1,),
        in_specs=[
            pl.BlockSpec((HALF_HEADS, 8, DH), lambda g: (half, 0, 0)),
            *[pl.BlockSpec((HALF_HEADS, DH, DH), lambda g: (0, 0, 0))] * len(parts),
        ],
        out_specs=pl.BlockSpec((HALF_HEADS, DH, DH), lambda g: (0, 0, 0)),
        out_shape=shape(BF16, HALF_HEADS, DH, DH),
        compiler_params=pltpu.CompilerParams(vmem_limit_bytes=VMEM_LIMIT),
        cost_estimate=pl.CostEstimate(flops=0, bytes_accessed=1 << 16, transcendentals=0),
    )(table, *parts)


def local_grad_kernel(
    core_ref, grad_ref, qkv_ref, state_ref, weights_ref, decay_ref, tall_ref,
    mine_ref, send_ref, dk_ref, dv_ref, dq_ref,
):
    core = core_ref[0]
    for j in range(GROUP):
        at = columns(j)
        grads = grad_ref[:, at]
        growth = jnp.exp(tall_ref[0, :, j : j + 1]) * SCALE
        scores = dot(grads, qkv_ref[2, :, at], COLS)
        grad_weights = (scores * decay_ref[j]).astype(BF16)
        rest = dot(grads, state_ref[j], COLS) * growth
        dq_ref[:, at] = (dot(grad_weights, qkv_ref[1, :, at], PLAIN) + rest).astype(BF16)
        dk_ref[:, at] = dot(grad_weights, qkv_ref[0, :, at], ROWS)
        dv_ref[:, at] = dot(weights_ref[j], grads, ROWS)
    mine_ref[0] = dq_ref[pl.ds(pl.multiple_of(core * TOK, TOK), TOK), :]
    send_ref[0] = dq_ref[pl.ds(pl.multiple_of((1 - core) * TOK, TOK), TOK), :]


def carried_grad_kernel(
    core_ref, table_ref, one_ref, two_ref, three_ref, theirs_ref, dk_in, dv_in, qkv_ref, tall_ref,
    _, _unread, mine_ref, send_ref, both_ref,
):
    core = core_ref[0]
    for j in range(GROUP):
        at = columns(j)
        state = weighted(table_ref[j], 0, one_ref[j], two_ref[j], three_ref[j], theirs_ref[j])
        run = tall_ref[0, :, j : j + 1]
        shrink = jnp.exp(run[SPAN - 1 :] - run) * SCALE
        keys = dk_in[:, at] + dot(qkv_ref[2, :, at], state, COLS) * shrink
        values = dv_in[:, at] + dot(qkv_ref[1, :, at], state, PLAIN) * shrink
        both_ref[0, :, at] = keys.astype(BF16)
        both_ref[1, :, at] = values.astype(BF16)
    for i in range(2):
        mine_ref[i] = both_ref[i, pl.ds(pl.multiple_of(core * TOK, TOK), TOK), :]
        send_ref[i] = both_ref[i, pl.ds(pl.multiple_of((1 - core) * TOK, TOK), TOK), :]


def carried_grads(half, core, table, received, dk, dv, qkv, tall, *unread):
    start = half * STEPS // 2
    tokens = pl.BlockSpec((SPAN, GROUP * DH), lambda g: (0, g + start))
    return per_heads(
        carried_grad_kernel,
        (core, table, *received, dk, dv, qkv, tall, *unread),
        [
            SCALARS,
            pl.BlockSpec((GROUP, 8, DH), lambda g: (g + start, 0, 0)),
            *[STATES] * 4,
            tokens,
            tokens,
            pl.BlockSpec((3, SPAN, GROUP * DH), lambda g: (0, 0, g + start)),
            pl.BlockSpec((1, SPAN, GROUP), lambda g: (g + start, 0, 0)),
            UNREAD,
            UNREAD,
        ],
        [shape(BF16, 2, TOK, HALF_HEADS * DH)] * 2,
        [HALVES] * 2,
        2 * HEADS * SPAN * DH * DH,
        [pltpu.VMEM((2, SPAN, GROUP * DH), BF16)],
        (STEPS // 2,),
    )


def project_kernel(place_ref, mixed_ref, *refs):
    core, y = place_ref[0], place_ref[1]
    blocks, quarters = refs[:5], refs[5:10]
    mine_x, send_x, mine_y, send_y, part_ref = refs[10:]
    mixed = mixed_ref[...]
    wide, quarter = blocks[0].shape[2], quarters[0].shape[1]
    middle = quarters[3].shape[0]

    def put(value, mine_ref, send_ref, at):
        part_ref[...] = value
        at = pl.multiple_of(at, DH)
        mine_ref[:, pl.ds(at, quarter)] = part_ref[pl.ds(pl.multiple_of(core * TOK, TOK), TOK), :]
        send = part_ref[pl.ds(pl.multiple_of((1 - core) * TOK, TOK), TOK), :]
        send_ref[:, pl.ds(at, quarter)] = send.astype(BF16)

    for i in range(wide // quarter):
        total = jnp.zeros((SPAN, quarter), F32)
        row = 0
        for block in blocks:
            part = block[:, :, i * quarter : (i + 1) * quarter].reshape(-1, quarter)
            total += dot(mixed[:, row : row + part.shape[0]], part, PLAIN)
            row += part.shape[0]
        put(total, mine_x, send_x, i * quarter)
    for step, part in ((0, quarters[0]), (3, quarters[1]), (1, quarters[2])):
        put(dot(mixed, part[...], PLAIN), mine_y, send_y, (y + step) % 4 * quarter)
    far = dot(mixed[:, :middle], quarters[3][...], PLAIN)
    far += dot(mixed[:, middle:], quarters[4][...], PLAIN)
    put(far, mine_y, send_y, (y + 2) % 4 * quarter)


def through_chips(state, theirs, flags, direction):
    pair = pl.pallas_call(
        pair_kernel,
        in_specs=[SCALARS, WHOLE, WHOLE],
        out_specs=WHOLE,
        out_shape=shape(BF16, HEADS + 1, DH, DH),
        compiler_params=pltpu.CompilerParams(vmem_limit_bytes=VMEM_LIMIT),
        cost_estimate=pl.CostEstimate(flops=0, bytes_accessed=1 << 16, transcendentals=0),
    )(flags, state, theirs)
    ring = shift(pair, dy=direction), shift(pair, dy=2), shift(pair, dy=-direction)
    return (theirs, *ring), pair


def shards(queries, key_rows, value_rows, log_decay, out_weight, out_grad):
    dp, ctx = lax.axis_index("dp"), lax.axis_index("ctx")
    z_low, x = dp // 4, dp % 4
    y, z_high, core = ctx // 4, (ctx // 2) % 2, ctx % 2
    width = out_weight.shape[1]
    wide, quarter = width * 2 // 3, width // 12

    steps = jnp.array([0, 3, 1, 2], jnp.int32)
    order = ((z_low + steps[None, :]) % 4 * 4 + (x + steps[:, None]) % 4).reshape(HEADS)
    heads = jnp.concatenate([2 * order + core, 2 * order + 1 - core]).astype(jnp.int32)
    place = heads * DH

    rows = lax.dynamic_slice_in_dim(out_weight, core * TOK, TOK, 0)
    part = lax.dynamic_slice_in_dim(rows, wide + y * quarter, quarter, 1)
    near = jnp.concatenate([part, shift(part, dz=1), shift(part, dz=-1), shift(part, dz=2)], 0)
    mine, other = split_heads(place, (queries[0], key_rows[0], value_rows[0]))
    near = after(near, other)
    plane = jnp.concatenate([near, shift(near, dx=1), shift(near, dx=-1), shift(near, dx=2)], 0)
    part = after(rows[:, :wide], near)
    half = TOK // 2
    opposite = jnp.concatenate([shift(part[:half], dz=2), shift(part[half:], dz=-2)], 0)
    column = jnp.stack([part, shift(part, dz=1), shift(part, dz=-1), opposite])

    plane = after(plane, column)
    y_before, y_behind = shift(plane, dy=1), shift(plane, dy=-1)

    qkv = join_tokens(core, mine, shift(after(other, plane), dcore=1), 1)
    grad_other = shift(after(out_grad[0], plane), dcore=1)
    qkv = after(qkv, grad_other)

    pick = (jnp.arange(2 * HEADS)[:, None] == heads[None, :]).astype(F32)
    gates = jnp.dot(log_decay[0], pick, precision=HIGHEST)
    gates = join_tokens(
        core, gates[:, :HEADS], shift(after(gates[:, HEADS:], plane), dcore=1)
    )
    places = jnp.arange(SPAN)
    lower = (places[:, None] >= places[None, :]).astype(F32)
    running = jnp.dot(lower, gates, precision=HIGHEST)
    wide_run = running.T.reshape(STEPS, GROUP, SPAN)
    tall_run = wide_run.transpose(0, 2, 1)
    sums = jnp.broadcast_to(running[SPAN - 1][:, None], (HEADS, DH))
    forward = jnp.stack([z_high == 0, y >= 1, y >= 2, y >= 3, z_high == 0]).astype(F32)
    backward = jnp.stack([z_high == 1, y <= 2, y <= 1, y <= 0, z_high == 1]).astype(F32)

    fresh = per_heads(
        fresh_kernel,
        (qkv, qkv, tall_run, sums),
        [
            pl.BlockSpec((1, SPAN, HEADS * DH), lambda g: (1, 0, 0)),
            pl.BlockSpec((1, SPAN, HEADS * DH), lambda g: (2, 0, 0)),
            pl.BlockSpec((STEPS, SPAN, GROUP), lambda g: (0, 0, 0)),
            pl.BlockSpec((HEADS, DH), lambda g: (0, 0)),
        ],
        shape(BF16, HEADS + 1, DH, DH),
        pl.BlockSpec((HEADS + 1, DH, DH), lambda g: (0, 0, 0)),
        2 * HEADS * SPAN * DH * DH,
        grid=(1,),
    )
    decay, weights = per_heads(
        weights_kernel,
        (after(qkv, fresh), tall_run, wide_run),
        [PACKED, TALL, WIDE],
        [shape(F32, HEADS, SPAN, SPAN), shape(BF16, HEADS, SPAN, SPAN)],
        [SQUARES, SQUARES],
        2 * HEADS * SPAN * SPAN * DH,
    )

    middle = plane.shape[0] // 2
    theirs = shift(fresh, dz=4)
    halves = after((y_before[:middle], y_behind[middle:]), fresh)
    weight_y = [
        plane, y_before, y_behind, shift(halves[0], dy=1), shift(halves[1], dy=-1)
    ]
    before, behind = shift(column, dx=1), shift(column, dx=-1)
    first, second = shift(before[:2], dx=1), shift(behind[2:], dx=-1)
    grad_rows = join_tokens(core, out_grad[0], grad_other)
    quarters = [
        lax.dynamic_slice_in_dim(grad_rows, wide + (y + step) % 4 * quarter, quarter, 1)
        for step in (0, 3, 1, 2)
    ]
    grad_columns = jnp.concatenate([grad_rows[:, :wide], *quarters], 1).T
    blocks = column, before, behind, first, second
    received, _ = through_chips(fresh, after(theirs, weights, *weight_y[3:]), forward, 1)

    table = pl.pallas_call(
        table_kernel,
        grid=(1,),
        in_specs=[SCALARS, *[SLAB] * 5],
        out_specs=pl.BlockSpec((HEADS, 8, DH), lambda g: (0, 0, 0)),
        out_shape=shape(F32, HEADS, 8, DH),
        cost_estimate=pl.CostEstimate(flops=0, bytes_accessed=1 << 16, transcendentals=0),
    )(backward, fresh, *received)

    grads, reach, reach_far = head_grads(grad_columns, blocks, weight_y, qkv, tall_run)
    theirs = shift(reach, dz=4)
    reach_far = after(reach_far, *received[1:])
    around = shift(reach_far, dy=-1), shift(reach_far, dy=2), shift(reach_far, dy=1)
    mixed, incoming = per_heads(
        mixed_kernel,
        (forward, *carried_operands(received), weights, qkv, tall_run, theirs),
        [SCALARS, *CARRIED, SQUARES, PACKED, TALL, UNREAD],
        [shape(BF16, SPAN, HEADS * DH), shape(BF16, HEADS, DH, DH)],
        [TOKENS, STATES],
        2 * HEADS * SPAN * (SPAN + DH) * DH,
    )
    pair = between(table, 0, reach, after(theirs, incoming))
    ring = shift(pair, dy=-1), shift(pair, dy=2), shift(pair, dy=1)
    passed = between(table, 1, reach_far, *after(around, incoming))
    crossed = shift(passed, dz=4)
    dq_mine, dq_send, dk, dv = per_heads(
        local_grad_kernel,
        (core[None], after(grads, pair, passed), qkv, incoming, weights, decay, tall_run),
        [SCALARS, TOKENS, PACKED, STATES, SQUARES, SQUARES, TALL],
        [
            *[shape(BF16, 1, TOK, HEADS * DH)] * 2,
            *[shape(F32, SPAN, HEADS * DH)] * 2,
        ],
        [HALF, HALF, TOKENS, TOKENS],
        2 * HEADS * SPAN * DH * (4 * SPAN + DH),
        [pltpu.VMEM((SPAN, GROUP * DH), BF16)],
    )

    mine_x, send_x, mine_y, send_y = pl.pallas_call(
        project_kernel,
        in_specs=[SCALARS, *[WHOLE] * 11],
        out_specs=[WHOLE] * 4,
        out_shape=[
            shape(F32, TOK, wide), shape(BF16, TOK, wide),
            shape(F32, TOK, width - wide), shape(BF16, TOK, width - wide),
        ],
        scratch_shapes=[pltpu.VMEM((SPAN, quarter), F32)],
        compiler_params=pltpu.CompilerParams(vmem_limit_bytes=VMEM_LIMIT),
        cost_estimate=pl.CostEstimate(flops=1 << 24, bytes_accessed=1 << 16, transcendentals=0),
    )(
        jnp.stack([core, y]),
        after(mixed, crossed),
        *blocks,
        *weight_y,
    )
    mine, send = carried_grads(
        0, core[None], table, (*ring, theirs), dk, dv, qkv, tall_run, send_y, dq_send
    )
    mine_far, send_far = carried_grads(
        1, core[None], table, (*around, crossed), dk, dv, qkv, tall_run, send_y, mine
    )
    query_grad, key_grad, value_grad = merge_heads(
        place,
        (dq_mine, mine, mine_far),
        (
            shift(after(dq_send, mine), dcore=1),
            shift(send, dcore=1),
            shift(send_far, dcore=1),
        ),
    )
    projected = jnp.concatenate(
        [
            mine_x + shift(after(send_x, mine), dcore=1).astype(F32),
            mine_y + shift(after(send_y, mine), dcore=1).astype(F32),
        ],
        1,
    ).astype(BF16)
    return projected[None], query_grad[None], key_grad[None], value_grad[None]


def solution(mesh):
    tokens = P("dp", "ctx", None)
    return jax.shard_map(
        shards,
        mesh=mesh,
        in_specs=(tokens, tokens, tokens, tokens, P("dp", None), tokens),
        out_specs=(tokens,) * 4,
        check_vma=False,
    )
```

```python
import jax
import jax.numpy as jnp
from jax import lax
from jax.experimental import pallas as pl
from jax.experimental.pallas import tpu as pltpu
from jax.sharding import PartitionSpec as P

AXES = ("dp", "ctx")
F32 = jnp.float32
BF16 = jnp.bfloat16
HIGHEST = lax.Precision.HIGHEST
DH = 128
SCALE = 1.0 / DH
TOK = 128
SPAN = 2 * TOK
HEADS = 16
GROUP = 2
HALF_HEADS = HEADS // 2
BAND = 4
STEPS = HEADS // GROUP
VMEM_LIMIT = 58 * 1024 * 1024


def device_place(x, y, z, core):
    return ((z % 4) * 4 + x) * 16 + y * 4 + (z // 4) * 2 + core


def moves(dx, dy, dz, dcore):
    pairs = []
    for x in range(4):
        for y in range(4):
            for z in range(8):
                for core in range(2):
                    target = ((x + dx) % 4, (y + dy) % 4, (z + dz) % 8, core ^ dcore)
                    pairs.append((device_place(x, y, z, core), device_place(*target)))
    return pairs


def shift(value, dx=0, dy=0, dz=0, dcore=0):
    return lax.ppermute(value, AXES, moves(dx, dy, dz, dcore))


def join_tokens(core, mine, other, axis=0):
    return jnp.where(
        core == 0,
        jnp.concatenate([mine, other], axis),
        jnp.concatenate([other, mine], axis),
    )


def dot(left, right, contract):
    return lax.dot_general(left, right, (contract, ((), ())), preferred_element_type=F32)


ROWS = ((0,), (0,))
PLAIN = ((1,), (0,))
COLS = ((1,), (1,))


def after(value, *others):
    return lax.optimization_barrier((value, *others))[0]


def split_kernel(place_ref, q_ref, k_ref, v_ref, mine_ref, other_ref):
    for h in range(HEADS):
        here = pl.ds(pl.multiple_of(place_ref[h], DH), DH)
        there = pl.ds(pl.multiple_of(place_ref[HEADS + h], DH), DH)
        for i, source in enumerate((q_ref, k_ref, v_ref)):
            mine_ref[i, :, columns(h)] = source[:, here]
            other_ref[i, :, columns(h)] = source[:, there]


def split_heads(place, arrays):
    return pl.pallas_call(
        split_kernel,
        in_specs=[SCALARS, *[WHOLE] * 3],
        out_specs=[WHOLE] * 2,
        out_shape=[shape(BF16, 3, TOK, HEADS * DH)] * 2,
        compiler_params=pltpu.CompilerParams(vmem_limit_bytes=VMEM_LIMIT),
        cost_estimate=pl.CostEstimate(flops=0, bytes_accessed=1 << 16, transcendentals=0),
    )(place, *arrays)


def merge_kernel(place_ref, *refs):
    mines, others, outs = refs[:3], refs[3:6], refs[6:]
    for h in range(HEADS):
        here = pl.ds(pl.multiple_of(place_ref[h], DH), DH)
        there = pl.ds(pl.multiple_of(place_ref[HEADS + h], DH), DH)
        half = columns(h % HALF_HEADS)
        for sources, at in ((mines, here), (others, there)):
            outs[0][:, at] = sources[0][0, :, columns(h)]
            for i in range(2):
                outs[1 + i][:, at] = sources[1 + h // HALF_HEADS][i, :, half]


def merge_heads(place, mines, others):
    return pl.pallas_call(
        merge_kernel,
        in_specs=[SCALARS, *[WHOLE] * 6],
        out_specs=[WHOLE] * 3,
        out_shape=[shape(BF16, TOK, 2 * HEADS * DH)] * 3,
        compiler_params=pltpu.CompilerParams(vmem_limit_bytes=VMEM_LIMIT),
        cost_estimate=pl.CostEstimate(flops=0, bytes_accessed=1 << 16, transcendentals=0),
    )(place, *mines, *others)


def columns(j):
    return slice(j * DH, (j + 1) * DH)


TOKENS = pl.BlockSpec((SPAN, GROUP * DH), lambda g: (0, g))
STATES = pl.BlockSpec((GROUP, DH, DH), lambda g: (g, 0, 0))
SQUARES = pl.BlockSpec((GROUP, SPAN, SPAN), lambda g: (g, 0, 0))
TALL = pl.BlockSpec((1, SPAN, GROUP), lambda g: (g, 0, 0))
WIDE = pl.BlockSpec((1, GROUP, SPAN), lambda g: (g, 0, 0))
PACKED = pl.BlockSpec((3, SPAN, GROUP * DH), lambda g: (0, 0, g))
HALVES = pl.BlockSpec((2, TOK, GROUP * DH), lambda g: (0, 0, g))
HALF = pl.BlockSpec((1, TOK, GROUP * DH), lambda g: (0, 0, g))
SLAB = pl.BlockSpec((1, DH, DH), lambda g: (HEADS, 0, 0))
WHOLE = pl.BlockSpec(memory_space=pltpu.VMEM)
SCALARS = pl.BlockSpec(memory_space=pltpu.SMEM)
UNREAD = pl.BlockSpec(memory_space=pl.ANY)


def shape(dtype, *dims):
    return jax.ShapeDtypeStruct(dims, dtype)


def per_heads(kernel, ins, specs, outs, out_specs, flops, scratch=(), grid=(STEPS,)):
    return pl.pallas_call(
        kernel,
        grid=grid,
        in_specs=specs,
        out_specs=out_specs,
        out_shape=outs,
        scratch_shapes=scratch,
        compiler_params=pltpu.CompilerParams(vmem_limit_bytes=VMEM_LIMIT),
        cost_estimate=pl.CostEstimate(flops=flops // 64, bytes_accessed=1 << 16, transcendentals=0),
    )(*ins)


def split_rows(value):
    high = value.astype(BF16)
    rest = value - high.astype(F32)
    middle = rest.astype(BF16)
    return high, middle, (rest - middle.astype(F32)).astype(BF16)


def put_sums(message_ref, *sums):
    message_ref[HEADS] = jnp.zeros((DH, DH), BF16)
    parts = [part for rows in sums for part in split_rows(rows)]
    for i, part in enumerate(parts):
        message_ref[HEADS, i * HEADS : (i + 1) * HEADS, :] = part


def sums_of(slab, which=0):
    starts = [(3 * which + i) * HEADS for i in range(3)]
    rows = [slab[start : start + HEADS, :].astype(F32) for start in starts]
    return rows[0] + rows[1] + rows[2]


def fresh_kernel(k_ref, v_ref, tall_ref, sums_ref, fresh_ref):
    for h in range(HEADS):
        run = tall_ref[h // GROUP, :, h % GROUP : h % GROUP + 1]
        shrink = jnp.exp(run[SPAN - 1 :] - run)
        keys = (k_ref[0, :, columns(h)].astype(F32) * shrink).astype(BF16)
        fresh_ref[h] = dot(keys, v_ref[0, :, columns(h)], ROWS).astype(BF16)
    put_sums(fresh_ref, sums_ref[...])


def weights_kernel(qkv_ref, tall_ref, wide_ref, decay_ref, weights_ref):
    later = lax.broadcasted_iota(jnp.int32, (SPAN, SPAN), 0)
    earlier = lax.broadcasted_iota(jnp.int32, (SPAN, SPAN), 1)
    causal = later >= earlier
    for j in range(GROUP):
        lag = tall_ref[0, :, j : j + 1] - wide_ref[0, j : j + 1, :]
        decay = jnp.where(causal, jnp.exp(jnp.where(causal, lag, 0.0)), 0.0) * SCALE
        decay_ref[j] = decay
        scores = dot(qkv_ref[0, :, columns(j)], qkv_ref[1, :, columns(j)], COLS)
        weights_ref[j] = (scores * decay).astype(BF16)


def pair_kernel(flags_ref, mine_ref, theirs_ref, pair_ref):
    ours, others = sums_of(mine_ref[HEADS]), sums_of(theirs_ref[HEADS])
    decays_mine = flags_ref[0] == 1.0
    mine_factor = jnp.where(decays_mine, jnp.exp(others), 1.0)
    theirs_factor = jnp.where(decays_mine, 1.0, jnp.exp(ours))
    for h in range(HEADS):
        mine = mine_ref[h].astype(F32) * mine_factor[h : h + 1]
        theirs = theirs_ref[h].astype(F32) * theirs_factor[h : h + 1]
        pair_ref[h] = (mine + theirs).astype(BF16)
    put_sums(
        pair_ref,
        jnp.where(decays_mine, ours, others),
        jnp.where(decays_mine, others, ours),
    )


def carried(flags_ref, head, j, theirs, one, two, three):
    wanted = lax.broadcasted_iota(jnp.int32, (HEADS, DH), 0) == head

    def row(slab_ref, count=1):
        sums = sum(sums_of(slab_ref[0], i) for i in range(count))
        return jnp.sum(jnp.where(wanted, sums, 0.0), axis=0, keepdims=True)

    (theirs_ref, theirs_slab), (one_ref, one_slab), (two_ref, two_slab) = theirs, one, two
    first, second = row(one_slab, 2), row(two_slab, 2)
    at_end = flags_ref[4] == 1.0
    last = jnp.where(at_end, 1.0, jnp.exp(row(theirs_slab)))
    total = one_ref[j].astype(F32) * flags_ref[1]
    total += two_ref[j].astype(F32) * (jnp.exp(first) * flags_ref[2])
    total += three[j].astype(F32) * (jnp.exp(first + second) * flags_ref[3])
    total = total * last + theirs_ref[j].astype(F32) * jnp.where(at_end, 0.0, 1.0)
    return total.astype(BF16)


CARRIED = [STATES, SLAB] * 3 + [STATES]


def carried_operands(received):
    theirs, one, two, three = received
    return theirs, theirs, one, one, two, two, three


def carried_refs(refs):
    return (refs[0], refs[1]), (refs[2], refs[3]), (refs[4], refs[5]), refs[6]


def mixed_kernel(flags_ref, *refs):
    weights_ref, qkv_ref, tall_ref, _, mixed_ref, state_ref = refs[7:]
    for j in range(GROUP):
        head = pl.program_id(0) * GROUP + j
        state = carried(flags_ref, head, j, *carried_refs(refs))
        state_ref[j] = state
        growth = jnp.exp(tall_ref[0, :, j : j + 1]) * SCALE
        intra = dot(weights_ref[j], qkv_ref[2, :, columns(j)], PLAIN)
        inter = dot(qkv_ref[0, :, columns(j)], state, PLAIN) * growth
        mixed_ref[:, columns(j)] = (intra + inter).astype(BF16)


def head_grad_kernel(og_ref, q_ref, tall_ref, *refs):
    blocks, quarters = refs[:5], refs[5:10]
    grad_ref, *reach_refs, wx_ref, wy_ref, sems = refs[10:]
    wide, quarter = wx_ref.shape[2], wy_ref.shape[2]
    size = BAND * DH

    def copies(band):
        if band < 3:
            pairs = [(blocks[band], wx_ref.at[band * BAND : (band + 1) * BAND])]
        else:
            half = BAND // 2
            starts = band * BAND, band * BAND + half
            pairs = [
                (block, wx_ref.at[start : start + half])
                for block, start in zip(blocks[3:], starts)
            ]
        rows = slice(band * size, (band + 1) * size)
        over = slice(band % 2 * size, (band % 2 + 1) * size)
        for i in range(3):
            pairs.append((quarters[i].at[rows], wy_ref.at[i, rows]))
        pairs.append((quarters[3 + band // 2].at[over], wy_ref.at[3, rows]))
        return [
            pltpu.make_async_copy(source, target, sems.at[band, i])
            for i, (source, target) in enumerate(pairs)
        ]

    bands = [copies(band) for band in range(HEADS // BAND)]
    for band in bands:
        for copy in band:
            copy.start()
    for band, waited in enumerate(bands):
        for copy in waited:
            copy.wait()
        rows = slice(band * size, (band + 1) * size)
        block = wx_ref[band * BAND : (band + 1) * BAND].reshape(size, wide)
        total = dot(block, og_ref[:wide], PLAIN)
        for i in range(4):
            at = wide + i * quarter
            total += dot(wy_ref[i, rows], og_ref[at : at + quarter], PLAIN)
        for i in range(BAND):
            head = band * BAND + i
            grads = total[columns(i)].T.astype(BF16)
            grad_ref[:, columns(head)] = grads
            run = tall_ref[head // GROUP, :, head % GROUP : head % GROUP + 1]
            queries = (q_ref[0, :, columns(head)].astype(F32) * jnp.exp(run)).astype(BF16)
            reach = dot(queries, grads, ROWS).astype(BF16)
            reach_refs[head // HALF_HEADS][head % HALF_HEADS] = reach


def head_grads(og, blocks, weight_y, qkv, tall):
    wide, quarter = blocks[0].shape[2], weight_y[0].shape[1]
    return pl.pallas_call(
        head_grad_kernel,
        grid=(1,),
        in_specs=[
            pl.BlockSpec(og.shape, lambda g: (0, 0)),
            pl.BlockSpec((1, SPAN, HEADS * DH), lambda g: (0, 0, 0)),
            pl.BlockSpec(tall.shape, lambda g: (0, 0, 0)),
            *[UNREAD] * 10,
        ],
        out_specs=[
            pl.BlockSpec((SPAN, HEADS * DH), lambda g: (0, 0)),
            *[pl.BlockSpec((HALF_HEADS, DH, DH), lambda g: (0, 0, 0))] * 2,
        ],
        out_shape=[
            shape(BF16, SPAN, HEADS * DH),
            *[shape(BF16, HALF_HEADS, DH, DH)] * 2,
        ],
        scratch_shapes=[
            pltpu.VMEM((HEADS, DH, wide), BF16),
            pltpu.VMEM((4, HEADS * DH, quarter), BF16),
            pltpu.SemaphoreType.DMA((HEADS // BAND, 6)),
        ],
        compiler_params=pltpu.CompilerParams(vmem_limit_bytes=VMEM_LIMIT),
        cost_estimate=pl.CostEstimate(flops=1 << 24, bytes_accessed=1 << 16, transcendentals=0),
    )(og, qkv, tall, *blocks, *weight_y)


def table_kernel(flags_ref, own_ref, theirs_ref, one_ref, two_ref, three_ref, table_ref):
    at_start = flags_ref[0] == 1.0
    own, other = sums_of(own_ref[0]), sums_of(theirs_ref[0])
    inner = [sums_of(ref[0], 0) for ref in (three_ref, two_ref, one_ref)]
    pairs = [rest + sums_of(ref[0], 1) for rest, ref in zip(inner, (three_ref, two_ref, one_ref))]
    valid = [flags_ref[i] for i in (1, 2, 3)]
    beyond = [jnp.zeros_like(own), pairs[0], pairs[0] + pairs[1]]
    zero, one = jnp.zeros_like(own), jnp.ones_like(own)
    last = jnp.where(at_start, one, jnp.exp(other))

    plain = [v * jnp.exp(log_sum) for v, log_sum in zip(valid, beyond)]
    first = [part * last for part in plain] + [jnp.where(at_start, zero, one)]
    first += [jnp.where(at_start, jnp.exp(other), one), jnp.where(at_start, one, jnp.exp(own))]

    through = [v * jnp.exp(log_sum + rest) for v, log_sum, rest in zip(valid, beyond, inner)]
    ring = [jnp.where(at_start, a, b) for a, b in zip(through, plain)]
    second = [part * last for part in ring] + [one, jnp.where(at_start, one, zero)]
    second += [part * jnp.where(at_start, jnp.exp(own), one) for part in ring]
    for h in range(HEADS):
        for i, rows in enumerate(first if h < HALF_HEADS else second):
            table_ref[h, i : i + 1, :] = rows[h : h + 1]


def weighted(table, first_row, *parts):
    total = None
    for i, part in enumerate(parts):
        term = part.astype(F32) * table[first_row + i : first_row + i + 1]
        total = term if total is None else total + term
    return total.astype(BF16)


def between_kernel(table_ref, *refs):
    *parts, out_ref = refs
    for h in range(HALF_HEADS):
        out_ref[h] = weighted(table_ref[h], 4, *[part[h] for part in parts])


def between(table, half, *parts):
    return pl.pallas_call(
        between_kernel,
        grid=(1,),
        in_specs=[
            pl.BlockSpec((HALF_HEADS, 8, DH), lambda g: (half, 0, 0)),
            *[pl.BlockSpec((HALF_HEADS, DH, DH), lambda g: (0, 0, 0))] * len(parts),
        ],
        out_specs=pl.BlockSpec((HALF_HEADS, DH, DH), lambda g: (0, 0, 0)),
        out_shape=shape(BF16, HALF_HEADS, DH, DH),
        compiler_params=pltpu.CompilerParams(vmem_limit_bytes=VMEM_LIMIT),
        cost_estimate=pl.CostEstimate(flops=0, bytes_accessed=1 << 16, transcendentals=0),
    )(table, *parts)


def local_grad_kernel(
    core_ref, grad_ref, qkv_ref, state_ref, weights_ref, decay_ref, tall_ref,
    mine_ref, send_ref, dk_ref, dv_ref, dq_ref,
):
    core = core_ref[0]
    for j in range(GROUP):
        at = columns(j)
        grads = grad_ref[:, at]
        growth = jnp.exp(tall_ref[0, :, j : j + 1]) * SCALE
        scores = dot(grads, qkv_ref[2, :, at], COLS)
        grad_weights = (scores * decay_ref[j]).astype(BF16)
        rest = dot(grads, state_ref[j], COLS) * growth
        dq_ref[:, at] = (dot(grad_weights, qkv_ref[1, :, at], PLAIN) + rest).astype(BF16)
        dk_ref[:, at] = dot(grad_weights, qkv_ref[0, :, at], ROWS)
        dv_ref[:, at] = dot(weights_ref[j], grads, ROWS)
    mine_ref[0] = dq_ref[pl.ds(pl.multiple_of(core * TOK, TOK), TOK), :]
    send_ref[0] = dq_ref[pl.ds(pl.multiple_of((1 - core) * TOK, TOK), TOK), :]


def carried_grad_kernel(
    core_ref, table_ref, one_ref, two_ref, three_ref, theirs_ref, dk_in, dv_in, qkv_ref, tall_ref,
    _, _unread, mine_ref, send_ref, both_ref,
):
    core = core_ref[0]
    for j in range(GROUP):
        at = columns(j)
        state = weighted(table_ref[j], 0, one_ref[j], two_ref[j], three_ref[j], theirs_ref[j])
        run = tall_ref[0, :, j : j + 1]
        shrink = jnp.exp(run[SPAN - 1 :] - run) * SCALE
        keys = dk_in[:, at] + dot(qkv_ref[2, :, at], state, COLS) * shrink
        values = dv_in[:, at] + dot(qkv_ref[1, :, at], state, PLAIN) * shrink
        both_ref[0, :, at] = keys.astype(BF16)
        both_ref[1, :, at] = values.astype(BF16)
    for i in range(2):
        mine_ref[i] = both_ref[i, pl.ds(pl.multiple_of(core * TOK, TOK), TOK), :]
        send_ref[i] = both_ref[i, pl.ds(pl.multiple_of((1 - core) * TOK, TOK), TOK), :]


def carried_grads(half, core, table, received, dk, dv, qkv, tall, *unread):
    start = half * STEPS // 2
    tokens = pl.BlockSpec((SPAN, GROUP * DH), lambda g: (0, g + start))
    return per_heads(
        carried_grad_kernel,
        (core, table, *received, dk, dv, qkv, tall, *unread),
        [
            SCALARS,
            pl.BlockSpec((GROUP, 8, DH), lambda g: (g + start, 0, 0)),
            *[STATES] * 4,
            tokens,
            tokens,
            pl.BlockSpec((3, SPAN, GROUP * DH), lambda g: (0, 0, g + start)),
            pl.BlockSpec((1, SPAN, GROUP), lambda g: (g + start, 0, 0)),
            UNREAD,
            UNREAD,
        ],
        [shape(BF16, 2, TOK, HALF_HEADS * DH)] * 2,
        [HALVES] * 2,
        2 * HEADS * SPAN * DH * DH,
        [pltpu.VMEM((2, SPAN, GROUP * DH), BF16)],
        (STEPS // 2,),
    )


def project_kernel(place_ref, mixed_ref, *refs):
    core, y = place_ref[0], place_ref[1]
    blocks, quarters = refs[:5], refs[5:10]
    mine_x, send_x, mine_y, send_y, part_ref = refs[10:]
    mixed = mixed_ref[...]
    wide, quarter = blocks[0].shape[2], quarters[0].shape[1]
    middle = quarters[3].shape[0]

    def put(value, mine_ref, send_ref, at):
        part_ref[...] = value
        at = pl.multiple_of(at, DH)
        mine_ref[:, pl.ds(at, quarter)] = part_ref[pl.ds(pl.multiple_of(core * TOK, TOK), TOK), :]
        send = part_ref[pl.ds(pl.multiple_of((1 - core) * TOK, TOK), TOK), :]
        send_ref[:, pl.ds(at, quarter)] = send.astype(BF16)

    for i in range(wide // quarter):
        total = jnp.zeros((SPAN, quarter), F32)
        row = 0
        for block in blocks:
            part = block[:, :, i * quarter : (i + 1) * quarter].reshape(-1, quarter)
            total += dot(mixed[:, row : row + part.shape[0]], part, PLAIN)
            row += part.shape[0]
        put(total, mine_x, send_x, i * quarter)
    for step, part in ((0, quarters[0]), (3, quarters[1]), (1, quarters[2])):
        put(dot(mixed, part[...], PLAIN), mine_y, send_y, (y + step) % 4 * quarter)
    far = dot(mixed[:, :middle], quarters[3][...], PLAIN)
    far += dot(mixed[:, middle:], quarters[4][...], PLAIN)
    put(far, mine_y, send_y, (y + 2) % 4 * quarter)


def through_chips(state, theirs, flags, direction):
    pair = pl.pallas_call(
        pair_kernel,
        in_specs=[SCALARS, WHOLE, WHOLE],
        out_specs=WHOLE,
        out_shape=shape(BF16, HEADS + 1, DH, DH),
        compiler_params=pltpu.CompilerParams(vmem_limit_bytes=VMEM_LIMIT),
        cost_estimate=pl.CostEstimate(flops=0, bytes_accessed=1 << 16, transcendentals=0),
    )(flags, state, theirs)
    ring = shift(pair, dy=direction), shift(pair, dy=2), shift(pair, dy=-direction)
    return (theirs, *ring), pair


def shards(queries, key_rows, value_rows, log_decay, out_weight, out_grad):
    dp, ctx = lax.axis_index("dp"), lax.axis_index("ctx")
    z_low, x = dp // 4, dp % 4
    y, z_high, core = ctx // 4, (ctx // 2) % 2, ctx % 2
    width = out_weight.shape[1]
    wide, quarter = width * 2 // 3, width // 12

    steps = jnp.array([0, 3, 1, 2], jnp.int32)
    order = ((z_low + steps[None, :]) % 4 * 4 + (x + steps[:, None]) % 4).reshape(HEADS)
    heads = jnp.concatenate([2 * order + core, 2 * order + 1 - core]).astype(jnp.int32)
    place = heads * DH

    rows = lax.dynamic_slice_in_dim(out_weight, core * TOK, TOK, 0)
    part = lax.dynamic_slice_in_dim(rows, wide + y * quarter, quarter, 1)
    near = jnp.concatenate([part, shift(part, dz=1), shift(part, dz=-1), shift(part, dz=2)], 0)
    mine, other = split_heads(place, (queries[0], key_rows[0], value_rows[0]))
    near = after(near, other)
    plane = jnp.concatenate([near, shift(near, dx=1), shift(near, dx=-1), shift(near, dx=2)], 0)
    part = after(rows[:, :wide], near)
    half = TOK // 2
    opposite = jnp.concatenate([shift(part[:half], dz=2), shift(part[half:], dz=-2)], 0)
    column = jnp.stack([part, shift(part, dz=1), shift(part, dz=-1), opposite])

    plane = after(plane, column)
    y_before, y_behind = shift(plane, dy=1), shift(plane, dy=-1)

    qkv = join_tokens(core, mine, shift(after(other, plane), dcore=1), 1)
    grad_other = shift(after(out_grad[0], plane), dcore=1)
    qkv = after(qkv, grad_other)

    pick = (jnp.arange(2 * HEADS)[:, None] == heads[None, :]).astype(F32)
    gates = jnp.dot(log_decay[0], pick, precision=HIGHEST)
    gates = join_tokens(
        core, gates[:, :HEADS], shift(after(gates[:, HEADS:], plane), dcore=1)
    )
    places = jnp.arange(SPAN)
    lower = (places[:, None] >= places[None, :]).astype(F32)
    running = jnp.dot(lower, gates, precision=HIGHEST)
    wide_run = running.T.reshape(STEPS, GROUP, SPAN)
    tall_run = wide_run.transpose(0, 2, 1)
    sums = jnp.broadcast_to(running[SPAN - 1][:, None], (HEADS, DH))
    forward = jnp.stack([z_high == 0, y >= 1, y >= 2, y >= 3, z_high == 0]).astype(F32)
    backward = jnp.stack([z_high == 1, y <= 2, y <= 1, y <= 0, z_high == 1]).astype(F32)

    fresh = per_heads(
        fresh_kernel,
        (qkv, qkv, tall_run, sums),
        [
            pl.BlockSpec((1, SPAN, HEADS * DH), lambda g: (1, 0, 0)),
            pl.BlockSpec((1, SPAN, HEADS * DH), lambda g: (2, 0, 0)),
            pl.BlockSpec((STEPS, SPAN, GROUP), lambda g: (0, 0, 0)),
            pl.BlockSpec((HEADS, DH), lambda g: (0, 0)),
        ],
        shape(BF16, HEADS + 1, DH, DH),
        pl.BlockSpec((HEADS + 1, DH, DH), lambda g: (0, 0, 0)),
        2 * HEADS * SPAN * DH * DH,
        grid=(1,),
    )
    decay, weights = per_heads(
        weights_kernel,
        (after(qkv, fresh), tall_run, wide_run),
        [PACKED, TALL, WIDE],
        [shape(F32, HEADS, SPAN, SPAN), shape(BF16, HEADS, SPAN, SPAN)],
        [SQUARES, SQUARES],
        2 * HEADS * SPAN * SPAN * DH,
    )

    middle = plane.shape[0] // 2
    theirs = shift(fresh, dz=4)
    halves = after((y_before[:middle], y_behind[middle:]), fresh)
    weight_y = [
        plane, y_before, y_behind, shift(halves[0], dy=1), shift(halves[1], dy=-1)
    ]
    before, behind = shift(column, dx=1), shift(column, dx=-1)
    halves = after((before[:2], behind[2:]), weights)
    first, second = shift(halves[0], dx=1), shift(halves[1], dx=-1)
    grad_rows = join_tokens(core, out_grad[0], grad_other)
    quarters = [
        lax.dynamic_slice_in_dim(grad_rows, wide + (y + step) % 4 * quarter, quarter, 1)
        for step in (0, 3, 1, 2)
    ]
    grad_columns = jnp.concatenate([grad_rows[:, :wide], *quarters], 1).T
    blocks = column, before, behind, first, second
    received, _ = through_chips(fresh, after(theirs, weights, *weight_y[3:]), forward, 1)

    table = pl.pallas_call(
        table_kernel,
        grid=(1,),
        in_specs=[SCALARS, *[SLAB] * 5],
        out_specs=pl.BlockSpec((HEADS, 8, DH), lambda g: (0, 0, 0)),
        out_shape=shape(F32, HEADS, 8, DH),
        cost_estimate=pl.CostEstimate(flops=0, bytes_accessed=1 << 16, transcendentals=0),
    )(backward, fresh, *received)

    grads, reach, reach_far = head_grads(grad_columns, blocks, weight_y, qkv, tall_run)
    theirs = shift(reach, dz=4)
    reach_far = after(reach_far, *received[1:])
    around = shift(reach_far, dy=-1), shift(reach_far, dy=2), shift(reach_far, dy=1)
    mixed, incoming = per_heads(
        mixed_kernel,
        (forward, *carried_operands(received), weights, qkv, tall_run, theirs),
        [SCALARS, *CARRIED, SQUARES, PACKED, TALL, UNREAD],
        [shape(BF16, SPAN, HEADS * DH), shape(BF16, HEADS, DH, DH)],
        [TOKENS, STATES],
        2 * HEADS * SPAN * (SPAN + DH) * DH,
    )
    pair = between(table, 0, reach, after(theirs, incoming))
    ring = shift(pair, dy=-1), shift(pair, dy=2), shift(pair, dy=1)
    passed = between(table, 1, reach_far, *after(around, incoming))
    crossed = shift(passed, dz=4)
    dq_mine, dq_send, dk, dv = per_heads(
        local_grad_kernel,
        (core[None], after(grads, pair, passed), qkv, incoming, weights, decay, tall_run),
        [SCALARS, TOKENS, PACKED, STATES, SQUARES, SQUARES, TALL],
        [
            *[shape(BF16, 1, TOK, HEADS * DH)] * 2,
            *[shape(F32, SPAN, HEADS * DH)] * 2,
        ],
        [HALF, HALF, TOKENS, TOKENS],
        2 * HEADS * SPAN * DH * (4 * SPAN + DH),
        [pltpu.VMEM((SPAN, GROUP * DH), BF16)],
    )

    mine_x, send_x, mine_y, send_y = pl.pallas_call(
        project_kernel,
        in_specs=[SCALARS, *[WHOLE] * 11],
        out_specs=[WHOLE] * 4,
        out_shape=[
            shape(F32, TOK, wide), shape(BF16, TOK, wide),
            shape(F32, TOK, width - wide), shape(BF16, TOK, width - wide),
        ],
        scratch_shapes=[pltpu.VMEM((SPAN, quarter), F32)],
        compiler_params=pltpu.CompilerParams(vmem_limit_bytes=VMEM_LIMIT),
        cost_estimate=pl.CostEstimate(flops=1 << 24, bytes_accessed=1 << 16, transcendentals=0),
    )(
        jnp.stack([core, y]),
        after(mixed, crossed),
        *blocks,
        *weight_y,
    )
    mine, send = carried_grads(
        0, core[None], table, (*ring, theirs), dk, dv, qkv, tall_run, send_y, dq_send
    )
    mine_far, send_far = carried_grads(
        1, core[None], table, (*around, crossed), dk, dv, qkv, tall_run, send_y, mine
    )
    query_grad, key_grad, value_grad = merge_heads(
        place,
        (dq_mine, mine, mine_far),
        (
            shift(after(dq_send, mine), dcore=1),
            shift(send, dcore=1),
            shift(send_far, dcore=1),
        ),
    )
    projected = jnp.concatenate(
        [
            mine_x + shift(after(send_x, mine), dcore=1).astype(F32),
            mine_y + shift(after(send_y, mine), dcore=1).astype(F32),
        ],
        1,
    ).astype(BF16)
    return projected[None], query_grad[None], key_grad[None], value_grad[None]


def solution(mesh):
    tokens = P("dp", "ctx", None)
    return jax.shard_map(
        shards,
        mesh=mesh,
        in_specs=(tokens, tokens, tokens, tokens, P("dp", None), tokens),
        out_specs=(tokens,) * 4,
        check_vma=False,
    )
```

```python
import jax
import jax.numpy as jnp
from jax import lax
from jax.experimental import pallas as pl
from jax.experimental.pallas import tpu as pltpu
from jax.sharding import PartitionSpec as P

AXES = ("dp", "ctx")
F32 = jnp.float32
BF16 = jnp.bfloat16
HIGHEST = lax.Precision.HIGHEST
DH = 128
SCALE = 1.0 / DH
TOK = 128
SPAN = 2 * TOK
HEADS = 16
GROUP = 2
HALF_HEADS = HEADS // 2
BAND = 4
STEPS = HEADS // GROUP
VMEM_LIMIT = 58 * 1024 * 1024


def device_place(x, y, z, core):
    return ((z % 4) * 4 + x) * 16 + y * 4 + (z // 4) * 2 + core


def moves(dx, dy, dz, dcore):
    pairs = []
    for x in range(4):
        for y in range(4):
            for z in range(8):
                for core in range(2):
                    target = ((x + dx) % 4, (y + dy) % 4, (z + dz) % 8, core ^ dcore)
                    pairs.append((device_place(x, y, z, core), device_place(*target)))
    return pairs


def shift(value, dx=0, dy=0, dz=0, dcore=0):
    return lax.ppermute(value, AXES, moves(dx, dy, dz, dcore))


def join_tokens(core, mine, other, axis=0):
    return jnp.where(
        core == 0,
        jnp.concatenate([mine, other], axis),
        jnp.concatenate([other, mine], axis),
    )


def dot(left, right, contract):
    return lax.dot_general(left, right, (contract, ((), ())), preferred_element_type=F32)


ROWS = ((0,), (0,))
PLAIN = ((1,), (0,))
COLS = ((1,), (1,))


def after(value, *others):
    return lax.optimization_barrier((value, *others))[0]


def split_kernel(place_ref, q_ref, k_ref, v_ref, mine_ref, other_ref):
    for h in range(HEADS):
        here = pl.ds(pl.multiple_of(place_ref[h], DH), DH)
        there = pl.ds(pl.multiple_of(place_ref[HEADS + h], DH), DH)
        for i, source in enumerate((q_ref, k_ref, v_ref)):
            mine_ref[i, :, columns(h)] = source[:, here]
            other_ref[i, :, columns(h)] = source[:, there]


def split_heads(place, arrays):
    return pl.pallas_call(
        split_kernel,
        in_specs=[SCALARS, *[WHOLE] * 3],
        out_specs=[WHOLE] * 2,
        out_shape=[shape(BF16, 3, TOK, HEADS * DH)] * 2,
        compiler_params=pltpu.CompilerParams(vmem_limit_bytes=VMEM_LIMIT),
        cost_estimate=pl.CostEstimate(flops=0, bytes_accessed=1 << 16, transcendentals=0),
    )(place, *arrays)


def merge_kernel(place_ref, *refs):
    mines, others, outs = refs[:3], refs[3:6], refs[6:]
    for h in range(HEADS):
        here = pl.ds(pl.multiple_of(place_ref[h], DH), DH)
        there = pl.ds(pl.multiple_of(place_ref[HEADS + h], DH), DH)
        half = columns(h % HALF_HEADS)
        for sources, at in ((mines, here), (others, there)):
            outs[0][:, at] = sources[0][0, :, columns(h)]
            for i in range(2):
                outs[1 + i][:, at] = sources[1 + h // HALF_HEADS][i, :, half]


def merge_heads(place, mines, others):
    return pl.pallas_call(
        merge_kernel,
        in_specs=[SCALARS, *[WHOLE] * 6],
        out_specs=[WHOLE] * 3,
        out_shape=[shape(BF16, TOK, 2 * HEADS * DH)] * 3,
        compiler_params=pltpu.CompilerParams(vmem_limit_bytes=VMEM_LIMIT),
        cost_estimate=pl.CostEstimate(flops=0, bytes_accessed=1 << 16, transcendentals=0),
    )(place, *mines, *others)


def columns(j):
    return slice(j * DH, (j + 1) * DH)


TOKENS = pl.BlockSpec((SPAN, GROUP * DH), lambda g: (0, g))
STATES = pl.BlockSpec((GROUP, DH, DH), lambda g: (g, 0, 0))
SQUARES = pl.BlockSpec((GROUP, SPAN, SPAN), lambda g: (g, 0, 0))
TALL = pl.BlockSpec((1, SPAN, GROUP), lambda g: (g, 0, 0))
WIDE = pl.BlockSpec((1, GROUP, SPAN), lambda g: (g, 0, 0))
PACKED = pl.BlockSpec((3, SPAN, GROUP * DH), lambda g: (0, 0, g))
HALVES = pl.BlockSpec((2, TOK, GROUP * DH), lambda g: (0, 0, g))
HALF = pl.BlockSpec((1, TOK, GROUP * DH), lambda g: (0, 0, g))
SLAB = pl.BlockSpec((1, DH, DH), lambda g: (HEADS, 0, 0))
WHOLE = pl.BlockSpec(memory_space=pltpu.VMEM)
SCALARS = pl.BlockSpec(memory_space=pltpu.SMEM)
UNREAD = pl.BlockSpec(memory_space=pl.ANY)


def shape(dtype, *dims):
    return jax.ShapeDtypeStruct(dims, dtype)


def per_heads(kernel, ins, specs, outs, out_specs, flops, scratch=(), grid=(STEPS,)):
    return pl.pallas_call(
        kernel,
        grid=grid,
        in_specs=specs,
        out_specs=out_specs,
        out_shape=outs,
        scratch_shapes=scratch,
        compiler_params=pltpu.CompilerParams(vmem_limit_bytes=VMEM_LIMIT),
        cost_estimate=pl.CostEstimate(flops=flops // 64, bytes_accessed=1 << 16, transcendentals=0),
    )(*ins)


def split_rows(value):
    high = value.astype(BF16)
    rest = value - high.astype(F32)
    middle = rest.astype(BF16)
    return high, middle, (rest - middle.astype(F32)).astype(BF16)


def put_sums(message_ref, *sums):
    message_ref[HEADS] = jnp.zeros((DH, DH), BF16)
    parts = [part for rows in sums for part in split_rows(rows)]
    for i, part in enumerate(parts):
        message_ref[HEADS, i * HEADS : (i + 1) * HEADS, :] = part


def sums_of(slab, which=0):
    starts = [(3 * which + i) * HEADS for i in range(3)]
    rows = [slab[start : start + HEADS, :].astype(F32) for start in starts]
    return rows[0] + rows[1] + rows[2]


def fresh_kernel(k_ref, v_ref, tall_ref, sums_ref, fresh_ref):
    for h in range(HEADS):
        run = tall_ref[h // GROUP, :, h % GROUP : h % GROUP + 1]
        shrink = jnp.exp(run[SPAN - 1 :] - run)
        keys = (k_ref[0, :, columns(h)].astype(F32) * shrink).astype(BF16)
        fresh_ref[h] = dot(keys, v_ref[0, :, columns(h)], ROWS).astype(BF16)
    put_sums(fresh_ref, sums_ref[...])


def weights_kernel(qkv_ref, tall_ref, wide_ref, decay_ref, weights_ref):
    later = lax.broadcasted_iota(jnp.int32, (SPAN, SPAN), 0)
    earlier = lax.broadcasted_iota(jnp.int32, (SPAN, SPAN), 1)
    causal = later >= earlier
    for j in range(GROUP):
        lag = tall_ref[0, :, j : j + 1] - wide_ref[0, j : j + 1, :]
        decay = jnp.where(causal, jnp.exp(jnp.where(causal, lag, 0.0)), 0.0) * SCALE
        decay_ref[j] = decay
        scores = dot(qkv_ref[0, :, columns(j)], qkv_ref[1, :, columns(j)], COLS)
        weights_ref[j] = (scores * decay).astype(BF16)


def pair_kernel(flags_ref, mine_ref, theirs_ref, pair_ref):
    ours, others = sums_of(mine_ref[HEADS]), sums_of(theirs_ref[HEADS])
    decays_mine = flags_ref[0] == 1.0
    mine_factor = jnp.where(decays_mine, jnp.exp(others), 1.0)
    theirs_factor = jnp.where(decays_mine, 1.0, jnp.exp(ours))
    for h in range(HEADS):
        mine = mine_ref[h].astype(F32) * mine_factor[h : h + 1]
        theirs = theirs_ref[h].astype(F32) * theirs_factor[h : h + 1]
        pair_ref[h] = (mine + theirs).astype(BF16)
    put_sums(
        pair_ref,
        jnp.where(decays_mine, ours, others),
        jnp.where(decays_mine, others, ours),
    )


def carried(flags_ref, head, j, theirs, one, two, three):
    wanted = lax.broadcasted_iota(jnp.int32, (HEADS, DH), 0) == head

    def row(slab_ref, count=1):
        sums = sum(sums_of(slab_ref[0], i) for i in range(count))
        return jnp.sum(jnp.where(wanted, sums, 0.0), axis=0, keepdims=True)

    (theirs_ref, theirs_slab), (one_ref, one_slab), (two_ref, two_slab) = theirs, one, two
    first, second = row(one_slab, 2), row(two_slab, 2)
    at_end = flags_ref[4] == 1.0
    last = jnp.where(at_end, 1.0, jnp.exp(row(theirs_slab)))
    total = one_ref[j].astype(F32) * flags_ref[1]
    total += two_ref[j].astype(F32) * (jnp.exp(first) * flags_ref[2])
    total += three[j].astype(F32) * (jnp.exp(first + second) * flags_ref[3])
    total = total * last + theirs_ref[j].astype(F32) * jnp.where(at_end, 0.0, 1.0)
    return total.astype(BF16)


CARRIED = [STATES, SLAB] * 3 + [STATES]


def carried_operands(received):
    theirs, one, two, three = received
    return theirs, theirs, one, one, two, two, three


def carried_refs(refs):
    return (refs[0], refs[1]), (refs[2], refs[3]), (refs[4], refs[5]), refs[6]


def mixed_kernel(flags_ref, *refs):
    weights_ref, qkv_ref, tall_ref, _, mixed_ref, state_ref = refs[7:]
    for j in range(GROUP):
        head = pl.program_id(0) * GROUP + j
        state = carried(flags_ref, head, j, *carried_refs(refs))
        state_ref[j] = state
        growth = jnp.exp(tall_ref[0, :, j : j + 1]) * SCALE
        intra = dot(weights_ref[j], qkv_ref[2, :, columns(j)], PLAIN)
        inter = dot(qkv_ref[0, :, columns(j)], state, PLAIN) * growth
        mixed_ref[:, columns(j)] = (intra + inter).astype(BF16)


def head_grad_kernel(og_ref, q_ref, tall_ref, *refs):
    blocks, quarters = refs[:5], refs[5:10]
    grad_ref, *reach_refs, wx_ref, wy_ref, sems = refs[10:]
    wide, quarter = wx_ref.shape[2], wy_ref.shape[2]
    size = BAND * DH

    def copies(band):
        if band < 3:
            pairs = [(blocks[band], wx_ref.at[band * BAND : (band + 1) * BAND])]
        else:
            half = BAND // 2
            starts = band * BAND, band * BAND + half
            pairs = [
                (block, wx_ref.at[start : start + half])
                for block, start in zip(blocks[3:], starts)
            ]
        rows = slice(band * size, (band + 1) * size)
        over = slice(band % 2 * size, (band % 2 + 1) * size)
        for i in range(3):
            pairs.append((quarters[i].at[rows], wy_ref.at[i, rows]))
        pairs.append((quarters[3 + band // 2].at[over], wy_ref.at[3, rows]))
        return [
            pltpu.make_async_copy(source, target, sems.at[band, i])
            for i, (source, target) in enumerate(pairs)
        ]

    bands = [copies(band) for band in range(HEADS // BAND)]
    for band in bands:
        for copy in band:
            copy.start()
    for band, waited in enumerate(bands):
        for copy in waited:
            copy.wait()
        rows = slice(band * size, (band + 1) * size)
        block = wx_ref[band * BAND : (band + 1) * BAND].reshape(size, wide)
        total = dot(block, og_ref[:wide], PLAIN)
        for i in range(4):
            at = wide + i * quarter
            total += dot(wy_ref[i, rows], og_ref[at : at + quarter], PLAIN)
        for i in range(BAND):
            head = band * BAND + i
            grads = total[columns(i)].T.astype(BF16)
            grad_ref[:, columns(head)] = grads
            run = tall_ref[head // GROUP, :, head % GROUP : head % GROUP + 1]
            queries = (q_ref[0, :, columns(head)].astype(F32) * jnp.exp(run)).astype(BF16)
            reach = dot(queries, grads, ROWS).astype(BF16)
            reach_refs[head // HALF_HEADS][head % HALF_HEADS] = reach


def head_grads(og, blocks, weight_y, qkv, tall):
    wide, quarter = blocks[0].shape[2], weight_y[0].shape[1]
    return pl.pallas_call(
        head_grad_kernel,
        grid=(1,),
        in_specs=[
            pl.BlockSpec(og.shape, lambda g: (0, 0)),
            pl.BlockSpec((1, SPAN, HEADS * DH), lambda g: (0, 0, 0)),
            pl.BlockSpec(tall.shape, lambda g: (0, 0, 0)),
            *[UNREAD] * 10,
        ],
        out_specs=[
            pl.BlockSpec((SPAN, HEADS * DH), lambda g: (0, 0)),
            *[pl.BlockSpec((HALF_HEADS, DH, DH), lambda g: (0, 0, 0))] * 2,
        ],
        out_shape=[
            shape(BF16, SPAN, HEADS * DH),
            *[shape(BF16, HALF_HEADS, DH, DH)] * 2,
        ],
        scratch_shapes=[
            pltpu.VMEM((HEADS, DH, wide), BF16),
            pltpu.VMEM((4, HEADS * DH, quarter), BF16),
            pltpu.SemaphoreType.DMA((HEADS // BAND, 6)),
        ],
        compiler_params=pltpu.CompilerParams(vmem_limit_bytes=VMEM_LIMIT),
        cost_estimate=pl.CostEstimate(flops=1 << 24, bytes_accessed=1 << 16, transcendentals=0),
    )(og, qkv, tall, *blocks, *weight_y)


def table_kernel(flags_ref, own_ref, theirs_ref, one_ref, two_ref, three_ref, table_ref):
    at_start = flags_ref[0] == 1.0
    own, other = sums_of(own_ref[0]), sums_of(theirs_ref[0])
    inner = [sums_of(ref[0], 0) for ref in (three_ref, two_ref, one_ref)]
    pairs = [rest + sums_of(ref[0], 1) for rest, ref in zip(inner, (three_ref, two_ref, one_ref))]
    valid = [flags_ref[i] for i in (1, 2, 3)]
    beyond = [jnp.zeros_like(own), pairs[0], pairs[0] + pairs[1]]
    zero, one = jnp.zeros_like(own), jnp.ones_like(own)
    last = jnp.where(at_start, one, jnp.exp(other))

    plain = [v * jnp.exp(log_sum) for v, log_sum in zip(valid, beyond)]
    first = [part * last for part in plain] + [jnp.where(at_start, zero, one)]
    first += [jnp.where(at_start, jnp.exp(other), one), jnp.where(at_start, one, jnp.exp(own))]

    through = [v * jnp.exp(log_sum + rest) for v, log_sum, rest in zip(valid, beyond, inner)]
    ring = [jnp.where(at_start, a, b) for a, b in zip(through, plain)]
    second = [part * last for part in ring] + [one, jnp.where(at_start, one, zero)]
    second += [part * jnp.where(at_start, jnp.exp(own), one) for part in ring]
    for h in range(HEADS):
        for i, rows in enumerate(first if h < HALF_HEADS else second):
            table_ref[h, i : i + 1, :] = rows[h : h + 1]


def weighted(table, first_row, *parts):
    total = None
    for i, part in enumerate(parts):
        term = part.astype(F32) * table[first_row + i : first_row + i + 1]
        total = term if total is None else total + term
    return total.astype(BF16)


def between_kernel(table_ref, *refs):
    *parts, out_ref = refs
    for h in range(HALF_HEADS):
        out_ref[h] = weighted(table_ref[h], 4, *[part[h] for part in parts])


def between(table, half, *parts):
    return pl.pallas_call(
        between_kernel,
        grid=(1,),
        in_specs=[
            pl.BlockSpec((HALF_HEADS, 8, DH), lambda g: (half, 0, 0)),
            *[pl.BlockSpec((HALF_HEADS, DH, DH), lambda g: (0, 0, 0))] * len(parts),
        ],
        out_specs=pl.BlockSpec((HALF_HEADS, DH, DH), lambda g: (0, 0, 0)),
        out_shape=shape(BF16, HALF_HEADS, DH, DH),
        compiler_params=pltpu.CompilerParams(vmem_limit_bytes=VMEM_LIMIT),
        cost_estimate=pl.CostEstimate(flops=0, bytes_accessed=1 << 16, transcendentals=0),
    )(table, *parts)


def local_grad_kernel(
    core_ref, grad_ref, qkv_ref, state_ref, weights_ref, decay_ref, tall_ref,
    mine_ref, send_ref, dk_ref, dv_ref, dq_ref,
):
    core = core_ref[0]
    for j in range(GROUP):
        at = columns(j)
        grads = grad_ref[:, at]
        growth = jnp.exp(tall_ref[0, :, j : j + 1]) * SCALE
        scores = dot(grads, qkv_ref[2, :, at], COLS)
        grad_weights = (scores * decay_ref[j]).astype(BF16)
        rest = dot(grads, state_ref[j], COLS) * growth
        dq_ref[:, at] = (dot(grad_weights, qkv_ref[1, :, at], PLAIN) + rest).astype(BF16)
        dk_ref[:, at] = dot(grad_weights, qkv_ref[0, :, at], ROWS)
        dv_ref[:, at] = dot(weights_ref[j], grads, ROWS)
    mine_ref[0] = dq_ref[pl.ds(pl.multiple_of(core * TOK, TOK), TOK), :]
    send_ref[0] = dq_ref[pl.ds(pl.multiple_of((1 - core) * TOK, TOK), TOK), :]


def carried_grad_kernel(
    core_ref, table_ref, one_ref, two_ref, three_ref, theirs_ref, dk_in, dv_in, qkv_ref, tall_ref,
    _, _unread, mine_ref, send_ref, both_ref,
):
    core = core_ref[0]
    for j in range(GROUP):
        at = columns(j)
        state = weighted(table_ref[j], 0, one_ref[j], two_ref[j], three_ref[j], theirs_ref[j])
        run = tall_ref[0, :, j : j + 1]
        shrink = jnp.exp(run[SPAN - 1 :] - run) * SCALE
        keys = dk_in[:, at] + dot(qkv_ref[2, :, at], state, COLS) * shrink
        values = dv_in[:, at] + dot(qkv_ref[1, :, at], state, PLAIN) * shrink
        both_ref[0, :, at] = keys.astype(BF16)
        both_ref[1, :, at] = values.astype(BF16)
    for i in range(2):
        mine_ref[i] = both_ref[i, pl.ds(pl.multiple_of(core * TOK, TOK), TOK), :]
        send_ref[i] = both_ref[i, pl.ds(pl.multiple_of((1 - core) * TOK, TOK), TOK), :]


def carried_grads(half, core, table, received, dk, dv, qkv, tall, *unread):
    start = half * STEPS // 2
    tokens = pl.BlockSpec((SPAN, GROUP * DH), lambda g: (0, g + start))
    return per_heads(
        carried_grad_kernel,
        (core, table, *received, dk, dv, qkv, tall, *unread),
        [
            SCALARS,
            pl.BlockSpec((GROUP, 8, DH), lambda g: (g + start, 0, 0)),
            *[STATES] * 4,
            tokens,
            tokens,
            pl.BlockSpec((3, SPAN, GROUP * DH), lambda g: (0, 0, g + start)),
            pl.BlockSpec((1, SPAN, GROUP), lambda g: (g + start, 0, 0)),
            UNREAD,
            UNREAD,
        ],
        [shape(BF16, 2, TOK, HALF_HEADS * DH)] * 2,
        [HALVES] * 2,
        2 * HEADS * SPAN * DH * DH,
        [pltpu.VMEM((2, SPAN, GROUP * DH), BF16)],
        (STEPS // 2,),
    )


def project_kernel(place_ref, mixed_ref, *refs):
    core, y = place_ref[0], place_ref[1]
    blocks, quarters = refs[:5], refs[5:10]
    mine_x, send_x, mine_y, send_y, part_ref = refs[10:]
    mixed = mixed_ref[...]
    wide, quarter = blocks[0].shape[2], quarters[0].shape[1]
    middle = quarters[3].shape[0]

    def put(value, mine_ref, send_ref, at):
        part_ref[...] = value
        at = pl.multiple_of(at, DH)
        mine_ref[:, pl.ds(at, quarter)] = part_ref[pl.ds(pl.multiple_of(core * TOK, TOK), TOK), :]
        send = part_ref[pl.ds(pl.multiple_of((1 - core) * TOK, TOK), TOK), :]
        send_ref[:, pl.ds(at, quarter)] = send.astype(BF16)

    for i in range(wide // quarter):
        total = jnp.zeros((SPAN, quarter), F32)
        row = 0
        for block in blocks:
            part = block[:, :, i * quarter : (i + 1) * quarter].reshape(-1, quarter)
            total += dot(mixed[:, row : row + part.shape[0]], part, PLAIN)
            row += part.shape[0]
        put(total, mine_x, send_x, i * quarter)
    for step, part in ((0, quarters[0]), (3, quarters[1]), (1, quarters[2])):
        put(dot(mixed, part[...], PLAIN), mine_y, send_y, (y + step) % 4 * quarter)
    far = dot(mixed[:, :middle], quarters[3][...], PLAIN)
    far += dot(mixed[:, middle:], quarters[4][...], PLAIN)
    put(far, mine_y, send_y, (y + 2) % 4 * quarter)


def through_chips(state, theirs, flags, direction):
    pair = pl.pallas_call(
        pair_kernel,
        in_specs=[SCALARS, WHOLE, WHOLE],
        out_specs=WHOLE,
        out_shape=shape(BF16, HEADS + 1, DH, DH),
        compiler_params=pltpu.CompilerParams(vmem_limit_bytes=VMEM_LIMIT),
        cost_estimate=pl.CostEstimate(flops=0, bytes_accessed=1 << 16, transcendentals=0),
    )(flags, state, theirs)
    ring = shift(pair, dy=direction), shift(pair, dy=2), shift(pair, dy=-direction)
    return (theirs, *ring), pair


def shards(queries, key_rows, value_rows, log_decay, out_weight, out_grad):
    dp, ctx = lax.axis_index("dp"), lax.axis_index("ctx")
    z_low, x = dp // 4, dp % 4
    y, z_high, core = ctx // 4, (ctx // 2) % 2, ctx % 2
    width = out_weight.shape[1]
    wide, quarter = width * 2 // 3, width // 12

    steps = jnp.array([0, 3, 1, 2], jnp.int32)
    order = ((z_low + steps[None, :]) % 4 * 4 + (x + steps[:, None]) % 4).reshape(HEADS)
    heads = jnp.concatenate([2 * order + core, 2 * order + 1 - core]).astype(jnp.int32)
    place = heads * DH

    rows = lax.dynamic_slice_in_dim(out_weight, core * TOK, TOK, 0)
    part = lax.dynamic_slice_in_dim(rows, wide + y * quarter, quarter, 1)
    near = jnp.concatenate([part, shift(part, dz=1), shift(part, dz=-1), shift(part, dz=2)], 0)
    mine, other = split_heads(place, (queries[0], key_rows[0], value_rows[0]))
    near = after(near, other)
    plane = jnp.concatenate([near, shift(near, dx=1), shift(near, dx=-1), shift(near, dx=2)], 0)
    part = after(rows[:, :wide], near)
    half = TOK // 2
    opposite = jnp.concatenate([shift(part[:half], dz=2), shift(part[half:], dz=-2)], 0)
    column = jnp.stack([part, shift(part, dz=1), shift(part, dz=-1), opposite])

    plane = after(plane, column)
    y_before, y_behind = shift(plane, dy=1), shift(plane, dy=-1)

    qkv = join_tokens(core, mine, shift(after(other, plane), dcore=1), 1)
    grad_other = shift(after(out_grad[0], plane), dcore=1)
    qkv = after(qkv, grad_other)

    pick = (jnp.arange(2 * HEADS)[:, None] == heads[None, :]).astype(F32)
    gates = jnp.dot(log_decay[0], pick, precision=HIGHEST)
    gates = join_tokens(
        core, gates[:, :HEADS], shift(after(gates[:, HEADS:], plane), dcore=1)
    )
    places = jnp.arange(SPAN)
    lower = (places[:, None] >= places[None, :]).astype(F32)
    running = jnp.dot(lower, gates, precision=HIGHEST)
    wide_run = running.T.reshape(STEPS, GROUP, SPAN)
    tall_run = wide_run.transpose(0, 2, 1)
    sums = jnp.broadcast_to(running[SPAN - 1][:, None], (HEADS, DH))
    forward = jnp.stack([z_high == 0, y >= 1, y >= 2, y >= 3, z_high == 0]).astype(F32)
    backward = jnp.stack([z_high == 1, y <= 2, y <= 1, y <= 0, z_high == 1]).astype(F32)

    fresh = per_heads(
        fresh_kernel,
        (qkv, qkv, tall_run, sums),
        [
            pl.BlockSpec((1, SPAN, HEADS * DH), lambda g: (1, 0, 0)),
            pl.BlockSpec((1, SPAN, HEADS * DH), lambda g: (2, 0, 0)),
            pl.BlockSpec((STEPS, SPAN, GROUP), lambda g: (0, 0, 0)),
            pl.BlockSpec((HEADS, DH), lambda g: (0, 0)),
        ],
        shape(BF16, HEADS + 1, DH, DH),
        pl.BlockSpec((HEADS + 1, DH, DH), lambda g: (0, 0, 0)),
        2 * HEADS * SPAN * DH * DH,
        grid=(1,),
    )
    decay, weights = per_heads(
        weights_kernel,
        (after(qkv, fresh), tall_run, wide_run),
        [PACKED, TALL, WIDE],
        [shape(F32, HEADS, SPAN, SPAN), shape(BF16, HEADS, SPAN, SPAN)],
        [SQUARES, SQUARES],
        2 * HEADS * SPAN * SPAN * DH,
    )

    middle = plane.shape[0] // 2
    theirs = shift(fresh, dz=4)
    halves = after((y_before[:middle], y_behind[middle:]), fresh)
    weight_y = [
        plane, y_before, y_behind, shift(halves[0], dy=1), shift(halves[1], dy=-1)
    ]
    before, behind = shift(column, dx=1), shift(column, dx=-1)
    halves = after((before[:2], behind[2:]), weights)
    first, second = shift(halves[0], dx=1), shift(halves[1], dx=-1)
    grad_rows = join_tokens(core, out_grad[0], grad_other)
    quarters = [
        lax.dynamic_slice_in_dim(grad_rows, wide + (y + step) % 4 * quarter, quarter, 1)
        for step in (0, 3, 1, 2)
    ]
    grad_columns = jnp.concatenate([grad_rows[:, :wide], *quarters], 1).T
    blocks = column, before, behind, first, second
    received, _ = through_chips(fresh, after(theirs, weights, *weight_y[3:]), forward, 1)

    table = pl.pallas_call(
        table_kernel,
        grid=(1,),
        in_specs=[SCALARS, *[SLAB] * 5],
        out_specs=pl.BlockSpec((HEADS, 8, DH), lambda g: (0, 0, 0)),
        out_shape=shape(F32, HEADS, 8, DH),
        cost_estimate=pl.CostEstimate(flops=0, bytes_accessed=1 << 16, transcendentals=0),
    )(backward, fresh, *received)

    grads, reach, reach_far = head_grads(grad_columns, blocks, weight_y, qkv, tall_run)
    theirs = shift(reach, dz=4)
    reach_far = after(reach_far, *received[1:])
    around = shift(reach_far, dy=-1), shift(reach_far, dy=2), shift(reach_far, dy=1)
    mixed, incoming = per_heads(
        mixed_kernel,
        (forward, *carried_operands(received), weights, qkv, tall_run, reach_far),
        [SCALARS, *CARRIED, SQUARES, PACKED, TALL, UNREAD],
        [shape(BF16, SPAN, HEADS * DH), shape(BF16, HEADS, DH, DH)],
        [TOKENS, STATES],
        2 * HEADS * SPAN * (SPAN + DH) * DH,
    )
    pair = between(table, 0, reach, after(theirs, incoming))
    ring = shift(pair, dy=-1), shift(pair, dy=2), shift(pair, dy=1)
    passed = between(table, 1, reach_far, *after(around, incoming))
    crossed = shift(passed, dz=4)
    dq_mine, dq_send, dk, dv = per_heads(
        local_grad_kernel,
        (core[None], after(grads, pair, passed), qkv, incoming, weights, decay, tall_run),
        [SCALARS, TOKENS, PACKED, STATES, SQUARES, SQUARES, TALL],
        [
            *[shape(BF16, 1, TOK, HEADS * DH)] * 2,
            *[shape(F32, SPAN, HEADS * DH)] * 2,
        ],
        [HALF, HALF, TOKENS, TOKENS],
        2 * HEADS * SPAN * DH * (4 * SPAN + DH),
        [pltpu.VMEM((SPAN, GROUP * DH), BF16)],
    )

    mine_x, send_x, mine_y, send_y = pl.pallas_call(
        project_kernel,
        in_specs=[SCALARS, *[WHOLE] * 11],
        out_specs=[WHOLE] * 4,
        out_shape=[
            shape(F32, TOK, wide), shape(BF16, TOK, wide),
            shape(F32, TOK, width - wide), shape(BF16, TOK, width - wide),
        ],
        scratch_shapes=[pltpu.VMEM((SPAN, quarter), F32)],
        compiler_params=pltpu.CompilerParams(vmem_limit_bytes=VMEM_LIMIT),
        cost_estimate=pl.CostEstimate(flops=1 << 24, bytes_accessed=1 << 16, transcendentals=0),
    )(
        jnp.stack([core, y]),
        after(mixed, crossed),
        *blocks,
        *weight_y,
    )
    mine, send = carried_grads(
        0, core[None], table, (*ring, theirs), dk, dv, qkv, tall_run, send_y, dq_send
    )
    mine_far, send_far = carried_grads(
        1, core[None], table, (*around, crossed), dk, dv, qkv, tall_run, send_y, mine
    )
    query_grad, key_grad, value_grad = merge_heads(
        place,
        (dq_mine, mine, mine_far),
        (
            shift(after(dq_send, mine), dcore=1),
            shift(send, dcore=1),
            shift(send_far, dcore=1),
        ),
    )
    projected = jnp.concatenate(
        [
            mine_x + shift(after(send_x, mine), dcore=1).astype(F32),
            mine_y + shift(after(send_y, mine), dcore=1).astype(F32),
        ],
        1,
    ).astype(BF16)
    return projected[None], query_grad[None], key_grad[None], value_grad[None]


def solution(mesh):
    tokens = P("dp", "ctx", None)
    return jax.shard_map(
        shards,
        mesh=mesh,
        in_specs=(tokens, tokens, tokens, tokens, P("dp", None), tokens),
        out_specs=(tokens,) * 4,
        check_vma=False,
    )
```
